256 devices in a mesh: prompt: 16 (over y, z_lo, core), resp: 16 (over z_hi, x).
Axes of the slice: x: 4, y: 4, z: 8 (z_hi: 4, z_lo: 2; z = z_hi * 2 + z_lo), core: 2. Of those that a mesh axis runs over, the one named last changes fastest.
Arguments:
- prefix_latent: bfloat16 [16, 256, 512], P('prompt', 'resp'), may hold values from -300 to 300
- prefix_rope: bfloat16 [16, 256, 64], P('prompt', 'resp'), may hold values from -600 to 600
- resp_latent: bfloat16 [16, 16, 80, 512], P('prompt', 'resp'), may hold values from -300 to 300
- resp_rope: bfloat16 [16, 16, 80, 64], P('prompt', 'resp'), may hold values from -6 to 6
- norm_gain: float32 [512], replicated, may hold values from 0.5 to 1.5
- queries: bfloat16 [16, 16, 80, 64, 576], P('prompt', 'resp'), may hold values from -6 to 6
- cotangent: bfloat16 [16, 16, 80, 64, 512], P('prompt', 'resp'), may hold values from -6 to 6
- lengths: int32 [16, 16], P('prompt', 'resp'), may hold values from 1 to 80, 800 in all within a row
- token_mask: int32 [16, 16, 80], P('prompt', 'resp'), may hold values 0 or 1
- rewards: float32 [16, 16], P('prompt', 'resp'), may hold values from -14 to 14
Outputs:
- grad_prefix_latent: float32 [16, 256, 512], P('prompt', 'resp')
- grad_prefix_rope: float32 [16, 256, 64], P('prompt', 'resp')
- grad_resp_latent: float32 [16, 16, 80, 512], P('prompt', 'resp')
- grad_resp_rope: float32 [16, 16, 80, 64], P('prompt', 'resp')
- grad_gain: float32 [512], replicated
The draws below stay inside these ranges and needn't reach their ends.
All inputs are finite; a program needn't handle non-finite values. No bound on the sum of `lengths` or of `token_mask` on one device may be relied on, other than what follows from the above.
Results may differ from the reference program's by a relative error of at most 0.017.
Values may be sent and summed in bfloat16 or wider, within the bound.
A program may use at most 64 MiB of HBM per device.

```python
import math
import jax
import jax.numpy as jnp
import numpy as np
from jax import lax

LAT = 512
ROPE = 64
HEADS = 64
PLEN = 256
RLEN = 80
PROMPTS = 16
NRESP = 16


def scaled_rows(key, shape, row_high):
    key_normal, key_rows, key_columns = jax.random.split(key, 3)
    normal = jnp.clip(jax.random.normal(key_normal, shape, jnp.float32), -5.0, 5.0)
    row_scale = jnp.exp(jax.random.uniform(key_rows, shape[:-1] + (1,), jnp.float32, math.log(0.3), math.log(row_high)))
    column_scale = jnp.exp(jax.random.uniform(key_columns, (shape[-1],), jnp.float32, math.log(0.3), math.log(3.0)))
    return row_scale * column_scale * normal


def draw_prefix_latent(key, part):
    key = jax.random.fold_in(key, 11)
    values = scaled_rows(key, (PROMPTS, PLEN, LAT), 3.0)
    return values.astype(jnp.bfloat16)


def draw_resp_latent(key, part):
    key = jax.random.fold_in(key, 12)
    values = scaled_rows(key, (PROMPTS, NRESP, RLEN, LAT), 3.0)
    return values.astype(jnp.bfloat16)


def draw_prefix_rope(key, part):
    key = jax.random.fold_in(key, 13)
    key_normal = jax.random.fold_in(key, 0)
    normal = jnp.clip(jax.random.normal(key_normal, (PROMPTS, PLEN, ROPE), jnp.float32), -4.0, 4.0)
    values = normal
    return values.astype(jnp.bfloat16)


def draw_rewards(key, part):
    key = jax.random.fold_in(key, 14)
    position = jnp.arange(NRESP, dtype=jnp.float32) / max(NRESP - 1, 1)
    values = (1.0 + 2.0 * position) * jnp.clip(jax.random.normal(key, (PROMPTS, NRESP), jnp.float32), -4.0, 4.0)
    return values


def plant(array, stream_key, least, largest):
    index_at = [jax.random.randint(jax.random.fold_in(stream_key, axis), (), 0, length) for axis, length in enumerate(array.shape)]
    widest = array.shape.index(max(array.shape))
    neighbour = index_at[:widest] + [(index_at[widest] + 1) % array.shape[widest]] + index_at[widest + 1:]
    return array.at[tuple(index_at)].set(least).at[tuple(neighbour)].set(largest)


def block_scale(own_key, dims, cuts, low, high):
    def one(axis_at, blocks):
        draws = jax.random.uniform(jax.random.fold_in(jax.random.fold_in(own_key, 6), axis_at), (blocks,), jnp.float32, low / len(cuts), high / len(cuts))
        return jnp.repeat(jnp.exp(draws), dims[axis_at] // blocks).reshape((-1,) + (1,) * (len(dims) - axis_at - 1))

    level = one(*cuts[0])
    for cut in cuts[1:]:
        level = level * one(*cut)
    return level


def profile(number_of, total, most, slope):
    portions = [(1 << 20) // math.isqrt(grade ** slope) + 1 for grade in range(2, number_of + 1)]
    spare, given = total - most - (number_of - 1), [1] * (number_of - 1)
    while spare > 0:
        free = [i for i in range(number_of - 1) if given[i] < most]
        pool, budget = sum([portions[i] for i in free]), spare
        for i in free:
            extra = min(most - given[i], max(1, budget * portions[i] // pool), spare)
            given[i] = given[i] + extra
            spare = spare - extra
    return np.array([most] + given)


def uneven(rng, amount, total, bound, lean):
    if amount == 2:
        one = jax.random.randint(rng, (), max(1, total - bound), min(bound, total - 1) + 1)
        return jnp.stack([one, total - one])
    tallies = jnp.asarray(profile(amount, total, bound, lean), jnp.int32)
    twos = (amount - 1) // 2
    giver, receiver = tallies[1:1 + 2 * twos:2], tallies[2:2 + 2 * twos:2]
    slack = jnp.minimum(giver - 1, bound - receiver)
    shifted = jax.random.randint(jax.random.fold_in(rng, 1), (twos,), 0, 1 << 20) % (slack + 1)
    tallies = tallies.at[1:1 + 2 * twos:2].set(giver - shifted).at[2:2 + 2 * twos:2].set(receiver + shifted)
    return tallies[jax.random.permutation(jax.random.fold_in(rng, 2), amount)]


def noise(stream_key, dims, deviation, most, cuts=(), kind=jnp.bfloat16):
    loudness = block_scale(stream_key, dims, cuts, -0.22, 0.18) if cuts else 1.0
    result = jax.random.normal(stream_key, dims, jnp.float32) * deviation * loudness
    return jnp.minimum(jnp.maximum(result, -most), most).astype(kind)


def setup_inputs(seed: int = 0) -> dict:
    key_of = jax.random.split(jax.random.key(seed), 11)
    prefix_latent = draw_prefix_latent(jax.random.fold_in(key_of[10], 71), 0)
    prefix_rope = draw_prefix_rope(jax.random.fold_in(key_of[10], 71), 0)
    resp_latent = draw_resp_latent(jax.random.fold_in(key_of[10], 71), 0)
    resp_rope = noise(key_of[3], (PROMPTS, NRESP, RLEN, ROPE), 1.0, 6.0, ((0, 16), (1, 16)))
    norm_gain = jnp.clip(1.0 + 0.1 * jax.random.normal(key_of[4], (LAT,), jnp.float32), 0.5, 1.5)
    queries = noise(key_of[5], (PROMPTS, NRESP, RLEN, HEADS, LAT + ROPE), 1.0, 6.0, ((0, 16), (1, 16)))
    cotangent = noise(key_of[6], (PROMPTS, NRESP, RLEN, HEADS, LAT), 1.0, 6.0, ((0, 16), (1, 16)))
    lengths = jax.vmap(lambda own: uneven(own, NRESP, NRESP * RLEN * 5 // 8, RLEN, 2))(jax.random.split(key_of[7], PROMPTS)).reshape((PROMPTS, NRESP)).astype(jnp.int32)
    token_mask = plant((jax.random.randint(key_of[8], (PROMPTS, NRESP, RLEN), 0, 4) < 3).astype(jnp.int32), jax.random.fold_in(key_of[8], 1), 0, 1)
    rewards = draw_rewards(jax.random.fold_in(key_of[10], 71), 0)
    return dict(prefix_latent=prefix_latent, prefix_rope=prefix_rope, resp_latent=resp_latent, resp_rope=resp_rope, norm_gain=norm_gain, queries=queries, cotangent=cotangent, lengths=lengths, token_mask=token_mask, rewards=rewards)


SOFTMAX_SCALE = 192.0 ** (-0.5)
NORM_EPSILON = 1e-06

def normalize(raw_rows, gain_vector):
    values = raw_rows.astype(jnp.float32)
    inverse = lax.rsqrt(lax.optimization_barrier(jnp.mean(values * values, axis=-1, keepdims=True)) + NORM_EPSILON)
    normed = values * inverse
    return (normed, inverse, (normed * gain_vector).astype(jnp.bfloat16))

def norm_backward(upstream, normed, inverse, gain_vector):
    scaled = upstream * gain_vector
    expected = lax.optimization_barrier(jnp.mean(scaled * normed, axis=-1, keepdims=True))
    gain_terms = lax.optimization_barrier(jnp.sum((upstream * normed).reshape(-1, normed.shape[-1]), axis=0))
    return ((scaled - normed * expected) * inverse, gain_terms)

def reference(prefix_latent, prefix_rope, resp_latent, resp_rope, norm_gain, queries, cotangent, lengths, token_mask, rewards):
    lat_width = prefix_latent.shape[-1]
    pre_normed, pre_inverse, pre_lat = normalize(prefix_latent, norm_gain)
    res_normed, res_inverse, res_lat = normalize(resp_latent, norm_gain)
    pre_keys = jnp.concatenate([pre_lat, prefix_rope], axis=-1)
    res_keys = jnp.concatenate([res_lat, resp_rope], axis=-1)
    advantage = rewards - lax.optimization_barrier(jnp.mean(rewards, axis=1, keepdims=True))
    positions = jnp.arange(RLEN)
    live_rows = (positions[None, None, :] < lengths[:, :, None]) & (token_mask > 0)
    weights = jnp.where(live_rows, -advantage[:, :, None], 0.0)
    grad_out = (weights[..., None, None] * cotangent.astype(jnp.float32)).astype(jnp.bfloat16)
    allowed = jnp.concatenate([jnp.ones((RLEN, PLEN), dtype=bool), positions[None, :] <= positions[:, None]], axis=1)
    highest = lax.Precision.HIGHEST

    def per_prompt(items):
        prefix_keys, prompt_queries, prompt_grads, prompt_keys = items

        def per_response(inner_items):
            query_rows, grad_rows, local_keys = inner_items
            key_rows = jnp.concatenate([prefix_keys, local_keys], axis=0)
            query_float = query_rows.astype(jnp.float32)
            grad_float = grad_rows.astype(jnp.float32)
            key_float = key_rows.astype(jnp.float32)
            scores = jnp.einsum('thd,kd->htk', query_float, key_float, precision=highest) * SOFTMAX_SCALE
            scores = jnp.where(allowed, scores, -jnp.inf)
            maximum = lax.optimization_barrier(jnp.max(scores, axis=-1, keepdims=True))
            exponent = jnp.exp(scores - maximum)
            softmax_rows = exponent / lax.optimization_barrier(jnp.sum(exponent, axis=-1, keepdims=True))
            grad_soft = jnp.einsum('the,ke->htk', grad_float, key_float[:, :lat_width], precision=highest)
            expected = lax.optimization_barrier(jnp.sum(softmax_rows * grad_soft, axis=-1, keepdims=True))
            grad_scores = (softmax_rows * (grad_soft - expected) * SOFTMAX_SCALE).astype(jnp.bfloat16)
            key_grads = jnp.einsum('htk,thd->kd', grad_scores.astype(jnp.float32), query_float, precision=highest)
            value_grads = jnp.einsum('htk,the->ke', softmax_rows.astype(jnp.bfloat16).astype(jnp.float32), grad_float, precision=highest)
            return (key_grads[:, :lat_width] + value_grads, key_grads[:, lat_width:])
        return lax.map(per_response, (prompt_queries, prompt_grads, prompt_keys))
    latent_grads, rope_grads = lax.map(per_prompt, (pre_keys, queries, grad_out, res_keys))
    prefix_latent_grad = lax.optimization_barrier(jnp.sum(latent_grads[:, :, :PLEN], axis=1))
    prefix_rope_grad = lax.optimization_barrier(jnp.sum(rope_grads[:, :, :PLEN], axis=1))
    grad_prefix_latent, gain_prefix = norm_backward(prefix_latent_grad, pre_normed, pre_inverse, norm_gain)
    grad_resp_latent, gain_local = norm_backward(latent_grads[:, :, PLEN:], res_normed, res_inverse, norm_gain)
    return (grad_prefix_latent, prefix_rope_grad, grad_resp_latent, rope_grads[:, :, PLEN:], gain_prefix + gain_local)
```

```python
import functools

import jax
import jax.numpy as jnp
from jax import lax
from jax.experimental import pallas as pl
from jax.experimental.pallas import tpu as pltpu
from jax.sharding import PartitionSpec as P

SOFTMAX_SCALE = 192.0 ** (-0.5)
LOG2E = 1.4426950408889634
NORM_EPSILON = 1e-06
NT = (((1,), (1,)), ((), ()))
LINE = 4
BLK = 512
MESH = pl.DeviceIdType.MESH
F32, BF16 = jnp.float32, jnp.bfloat16


def normed_rows(raw):
    values = raw.astype(F32)
    inverse = lax.rsqrt(jnp.mean(values * values, axis=-1, keepdims=True) + NORM_EPSILON)
    return values * inverse, inverse


def norm_backward(upstream, normed, inverse, gain):
    scaled = upstream * gain
    expected = jnp.mean(scaled * normed, axis=-1, keepdims=True)
    return (scaled - normed * expected) * inverse


def kernel(
    prompts,
    pl_hbm, pr_hbm, rl_hbm, rr_hbm, gain_hbm, q_hbm, c_hbm, len_hbm, mask_hbm, rew_hbm,
    o_pl, o_pr, o_rl, o_rr, o_gain,
    q_v, c_v, p_st, d_st, keys, normed, gathered, pl_v, pr_v, rl_v, rr_v, gain_v,
    len_s, mask_s, rew_s, acc, send_x, recv_x, send_z, recv_z, sum_z,
    gain_own, gain_x, gain_xs, gain_z, gain_zs, gain_p,
    load_sem, g_send, g_recv, x_send, x_recv, z_send, z_recv, gx_send, gx_recv,
    gz_send, gz_recv, gp_send, gp_recv,
):
    rows, lat = c_v.shape
    wide = q_v.shape[1]
    rope = wide - lat
    local = rl_v.shape[0]
    own = pl_v.shape[0]
    plen = own * LINE * LINE
    group = own * LINE

    me = lax.axis_index("resp")
    prompt = lax.axis_index("prompt")
    my_z, my_x = me // LINE, lax.rem(me, LINE)

    small = [
        pltpu.make_async_copy(src, dst, load_sem.at[i])
        for i, (src, dst) in enumerate(
            ((pl_hbm, pl_v), (pr_hbm, pr_v), (rew_hbm, rew_s), (rl_hbm, rl_v), (rr_hbm, rr_v),
             (gain_hbm, gain_v), (len_hbm, len_s), (mask_hbm, mask_s))
        )
    ]
    for copy in small:
        copy.start()

    def on_x(step):
        return lax.rem(my_x + step, LINE)

    def on_z(step):
        return lax.rem(my_z + step, LINE)

    barrier = pltpu.get_barrier_semaphore()
    for step in range(1, LINE):
        pl.semaphore_signal(barrier, inc=1, device_id={"resp": my_z * LINE + on_x(step)}, device_id_type=MESH)
        pl.semaphore_signal(barrier, inc=1, device_id={"resp": on_z(step) * LINE + my_x}, device_id_type=MESH)
    for step in range(1, prompts):
        pl.semaphore_signal(barrier, inc=1, device_id={"prompt": lax.rem(prompt + step, prompts)}, device_id_type=MESH)
    big = [
        pltpu.make_async_copy(q_hbm, q_v, load_sem.at[8]),
        pltpu.make_async_copy(c_hbm, c_v, load_sem.at[9]),
    ]
    for copy in big:
        copy.start()
    for copy in small[:3]:
        copy.wait()

    reward = jnp.full((own, rope), rew_s[0, 0], F32)
    high = reward.astype(BF16)
    rest = reward - high.astype(F32)
    mid = rest.astype(BF16)
    low = (rest - mid.astype(F32)).astype(BF16)
    lane = lax.broadcasted_iota(jnp.int32, (own, rope), 1)
    terms = jnp.where(
        lane == 0, high.astype(F32), jnp.where(lane == 1, mid.astype(F32), jnp.where(lane == 2, low.astype(F32), 0.0))
    )
    mine = gathered.at[my_x, my_z]
    mine[:, :lat] = pl_v[...]
    mine[:, lat:] = jnp.concatenate([pr_v[...].astype(F32), terms], axis=1).astype(BF16)

    pl.semaphore_wait(barrier, 2 * (LINE - 1) + prompts - 1)
    along_z = []
    for step in range(1, LINE):
        copy = pltpu.make_async_remote_copy(
            src_ref=gathered.at[my_x, my_z], dst_ref=gathered.at[my_x, my_z],
            send_sem=g_send.at[step], recv_sem=g_recv.at[step],
            device_id={"resp": on_z(step) * LINE + my_x}, device_id_type=MESH,
        )
        copy.start()
        along_z.append(copy)

    for copy in small[3:]:
        copy.wait()
    gain = gain_v[...]
    res_normed, res_inverse = normed_rows(rl_v[...])
    normed[plen:, :] = res_normed
    keys[plen:, :lat] = (res_normed * gain).astype(BF16)
    eye = (
        lax.broadcasted_iota(jnp.int32, (local, local), 0) == lax.broadcasted_iota(jnp.int32, (local, local), 1)
    ).astype(F32).astype(BF16)
    keys[plen:, lat:] = lax.dot_general(eye, rr_v[...], NT, preferred_element_type=F32).astype(BF16)

    for copy in along_z:
        copy.wait()
    along_x = []
    for step in range(1, LINE):
        copy = pltpu.make_async_remote_copy(
            src_ref=gathered.at[my_x], dst_ref=gathered.at[my_x],
            send_sem=g_send.at[LINE + step], recv_sem=g_recv.at[LINE + step],
            device_id={"resp": my_z * LINE + on_x(step)}, device_id_type=MESH,
        )
        copy.start()
        along_x.append(copy)
    for copy in along_x:
        copy.wait()

    raw = gathered[...].reshape(plen, lat + 2 * rope)
    pre_normed, pre_inverse = normed_rows(raw[:, :lat])
    normed[:plen, :] = pre_normed
    keys[:plen, :lat] = (pre_normed * gain).astype(BF16)
    keys[:plen, lat:] = raw[:, lat : lat + rope]
    reward_sum = jnp.sum(raw[:, lat:].astype(F32)[:, rope:]) / own
    factor = reward_sum / (LINE * LINE) - rew_s[0, 0]

    for copy in big:
        copy.wait()
    heads = rows // local
    per_block = BLK // heads
    column = lax.broadcasted_iota(jnp.int32, (1, BLK), 1)
    key_at = lax.broadcasted_iota(jnp.int32, (local, BLK), 0)
    token_in = lax.broadcasted_iota(jnp.int32, (local, BLK), 1) // heads
    length = len_s[0, 0]

    def forward(block, carry):
        at = pl.ds(pl.multiple_of(block * BLK, BLK), BLK)
        first = block * per_block
        live = jnp.zeros((1, BLK), F32)
        for i in range(per_block):
            weight = jnp.where((first + i < length) & (mask_s[0, first + i] > 0), 1.0, 0.0)
            live = jnp.where((column >= i * heads) & (column < (i + 1) * heads), weight, live)
        scores = lax.dot_general(keys[...], q_v[at, :], NT, preferred_element_type=F32)
        grad_soft = lax.dot_general(keys[:, :lat], c_v[at, :], NT, preferred_element_type=F32)
        visible = key_at <= token_in + first
        scores = jnp.concatenate([scores[:plen], jnp.where(visible, scores[plen:], -jnp.inf)], axis=0)
        maximum = jnp.max(scores, axis=0, keepdims=True)
        powers = jnp.exp2((scores - maximum) * (SOFTMAX_SCALE * LOG2E))
        inverse = 1.0 / jnp.sum(powers, axis=0, keepdims=True)
        expected = jnp.sum(powers * grad_soft, axis=0, keepdims=True) * inverse
        soft = powers * (inverse * live)
        p_st[:, at] = soft.astype(BF16)
        d_st[:, at] = (soft * (grad_soft - expected)).astype(BF16)
        return carry

    lax.fori_loop(0, rows // BLK, forward, 0)

    def contract(stored, values, lo, hi):
        return jnp.dot(stored[...], values[:, lo:hi], preferred_element_type=F32)

    parts = ((0, 256), (256, 512), (512, 576))
    x_copies, gain_copies = [], []
    for part, (lo, hi) in enumerate(parts):
        total = contract(d_st, q_v, lo, hi) * SOFTMAX_SCALE
        if hi <= lat:
            total = total + contract(p_st, c_v, lo, hi)
        total = total * factor
        acc[:, lo:hi] = total
        send_x[:, :, lo:hi] = total[:plen].astype(BF16).reshape(LINE, group, hi - lo)
        started = []
        for step in range(1, LINE):
            copy = pltpu.make_async_remote_copy(
                src_ref=send_x.at[on_x(step), :, lo:hi], dst_ref=recv_x.at[step, :, lo:hi],
                send_sem=x_send.at[part, step], recv_sem=x_recv.at[part, step],
                device_id={"resp": my_z * LINE + on_x(step)}, device_id_type=MESH,
            )
            copy.start()
            started.append(copy)
        x_copies.append(started)
        if hi <= lat:
            gain_own[:, lo:hi] = jnp.sum(total * normed[:, lo:hi], axis=0, keepdims=True)

    for step in range(1, LINE):
        copy = pltpu.make_async_remote_copy(
            src_ref=gain_own, dst_ref=gain_x.at[step],
            send_sem=gx_send.at[step], recv_sem=gx_recv.at[step],
            device_id={"resp": my_z * LINE + on_x(step)}, device_id_type=MESH,
        )
        copy.start()
        gain_copies.append(copy)

    z_copies = []
    mine_rows = pl.ds(pl.multiple_of(my_x * group, group), group)
    for part, (lo, hi) in enumerate(parts):
        for copy in x_copies[part]:
            copy.wait()
        total = acc[mine_rows, lo:hi]
        for step in range(1, LINE):
            total = total + recv_x[step, :, lo:hi].astype(F32)
        sum_z[:, :, lo:hi] = total.reshape(LINE, own, hi - lo)
        send_z[:, :, lo:hi] = total.astype(BF16).reshape(LINE, own, hi - lo)
        started = []
        for step in range(1, LINE):
            copy = pltpu.make_async_remote_copy(
                src_ref=send_z.at[on_z(step), :, lo:hi], dst_ref=recv_z.at[step, :, lo:hi],
                send_sem=z_send.at[part, step], recv_sem=z_recv.at[part, step],
                device_id={"resp": on_z(step) * LINE + my_x}, device_id_type=MESH,
            )
            copy.start()
            started.append(copy)
        z_copies.append(started)

    for copy in gain_copies:
        copy.wait()
    total_gain = gain_own[...]
    for step in range(1, LINE):
        total_gain = total_gain + gain_x[step]
    gain_xs[...] = total_gain
    gain_copies = []
    for step in range(1, LINE):
        copy = pltpu.make_async_remote_copy(
            src_ref=gain_xs, dst_ref=gain_z.at[step],
            send_sem=gz_send.at[step], recv_sem=gz_recv.at[step],
            device_id={"resp": on_z(step) * LINE + my_x}, device_id_type=MESH,
        )
        copy.start()
        gain_copies.append(copy)

    o_rl[...] = norm_backward(acc[plen:, :lat], res_normed, res_inverse, gain)
    o_rr[...] = acc[plen:, lat:].T

    for copy in gain_copies:
        copy.wait()
    total_gain = gain_xs[...]
    for step in range(1, LINE):
        total_gain = total_gain + gain_z[step]
    gain_zs[...] = total_gain
    gain_copies = []
    for step in range(1, prompts):
        copy = pltpu.make_async_remote_copy(
            src_ref=gain_zs, dst_ref=gain_p.at[step],
            send_sem=gp_send.at[step], recv_sem=gp_recv.at[step],
            device_id={"prompt": lax.rem(prompt + step, prompts)}, device_id_type=MESH,
        )
        copy.start()
        gain_copies.append(copy)

    for started in z_copies:
        for copy in started:
            copy.wait()
    total = sum_z[my_z]
    for step in range(1, LINE):
        total = total + recv_z[step].astype(F32)
    own_normed, own_inverse = normed_rows(pl_v[...])
    o_pl[...] = norm_backward(total[:, :lat], own_normed, own_inverse, gain)
    o_pr[...] = total[:, lat:]

    for copy in gain_copies:
        copy.wait()
    total_gain = gain_zs[...]
    for step in range(1, prompts):
        total_gain = total_gain + gain_p[step]
    o_gain[...] = total_gain


def per_device(
    prompts, prefix_latent, prefix_rope, resp_latent, resp_rope, norm_gain, queries, cotangent, lengths, token_mask, rewards
):
    tokens, heads, wide = queries.shape[2:]
    lat = cotangent.shape[-1]
    rope = wide - lat
    own = prefix_latent.shape[1]
    rows = tokens * heads
    plen = own * LINE * LINE
    count = plen + tokens
    dma = pltpu.SemaphoreType.DMA
    out = pl.pallas_call(
        functools.partial(kernel, prompts),
        out_shape=(
            jax.ShapeDtypeStruct((own, lat), F32),
            jax.ShapeDtypeStruct((own, rope), F32),
            jax.ShapeDtypeStruct((tokens, lat), F32),
            jax.ShapeDtypeStruct((rope, tokens), F32),
            jax.ShapeDtypeStruct((1, lat), F32),
        ),
        in_specs=[pl.BlockSpec(memory_space=pl.ANY)] * 10,
        out_specs=[pl.BlockSpec(memory_space=pltpu.VMEM)] * 5,
        scratch_shapes=[
            pltpu.VMEM((rows, wide), BF16),
            pltpu.VMEM((rows, lat), BF16),
            pltpu.VMEM((count, rows), BF16),
            pltpu.VMEM((count, rows), BF16),
            pltpu.VMEM((count, wide), BF16),
            pltpu.VMEM((count, lat), F32),
            pltpu.VMEM((LINE, LINE, own, lat + 2 * rope), BF16),
            pltpu.VMEM((own, lat), BF16),
            pltpu.VMEM((own, rope), BF16),
            pltpu.VMEM((tokens, lat), BF16),
            pltpu.VMEM((rope, tokens), BF16),
            pltpu.VMEM((1, lat), F32),
            pltpu.SMEM((1, 1), jnp.int32),
            pltpu.SMEM((1, tokens), jnp.int32),
            pltpu.SMEM((1, 1), F32),
            pltpu.VMEM((count, wide), F32),
            pltpu.VMEM((LINE, own * LINE, wide), BF16),
            pltpu.VMEM((LINE, own * LINE, wide), BF16),
            pltpu.VMEM((LINE, own, wide), BF16),
            pltpu.VMEM((LINE, own, wide), BF16),
            pltpu.VMEM((LINE, own, wide), F32),
            pltpu.VMEM((1, lat), F32),
            pltpu.VMEM((LINE, 1, lat), F32),
            pltpu.VMEM((1, lat), F32),
            pltpu.VMEM((LINE, 1, lat), F32),
            pltpu.VMEM((1, lat), F32),
            pltpu.VMEM((prompts, 1, lat), F32),
            dma((10,)),
            dma((2 * LINE,)),
            dma((2 * LINE,)),
            dma((3, LINE)),
            dma((3, LINE)),
            dma((3, LINE)),
            dma((3, LINE)),
            dma((LINE,)),
            dma((LINE,)),
            dma((LINE,)),
            dma((LINE,)),
            dma((prompts,)),
            dma((prompts,)),
        ],
        compiler_params=pltpu.CompilerParams(
            collective_id=0, has_side_effects=True, vmem_limit_bytes=56 * 2**20
        ),
        name="grpo_backward",
    )(
        prefix_latent[0],
        prefix_rope[0],
        resp_latent[0, 0],
        resp_rope[0, 0].T,
        norm_gain[None],
        queries.reshape(rows, wide),
        cotangent.reshape(rows, lat),
        lengths,
        token_mask[0],
        rewards,
    )
    return (out[0][None], out[1][None], out[2][None, None], out[3].T[None, None], out[4][0])


def solution(mesh):
    placed = (
        P("prompt", "resp", None),
        P("prompt", "resp", None),
        P("prompt", "resp", None, None),
        P("prompt", "resp", None, None),
        P(),
        P("prompt", "resp", None, None, None),
        P("prompt", "resp", None, None, None),
        P("prompt", "resp"),
        P("prompt", "resp", None),
        P("prompt", "resp"),
    )
    return jax.shard_map(
        functools.partial(per_device, mesh.shape["prompt"]),
        mesh=mesh,
        in_specs=placed,
        out_specs=(
            P("prompt", "resp", None),
            P("prompt", "resp", None),
            P("prompt", "resp", None, None),
            P("prompt", "resp", None, None),
            P(),
        ),
        check_vma=False,
    )
```

```python
import jax
import jax.numpy as jnp
from jax import lax
from jax.experimental import pallas as pl
from jax.experimental.pallas import tpu as pltpu
from jax.sharding import PartitionSpec as P

SOFTMAX_SCALE = 192.0 ** (-0.5)
LOG2E = 1.4426950408889634
NORM_EPSILON = 1e-06
NT = (((1,), (1,)), ((), ()))
LINE = 4
BLK = 512
UNROLL = 5
MESH = pl.DeviceIdType.MESH
F32, BF16 = jnp.float32, jnp.bfloat16


def normed_rows(raw):
    values = raw.astype(F32)
    inverse = lax.rsqrt(jnp.mean(values * values, axis=-1, keepdims=True) + NORM_EPSILON)
    return values * inverse, inverse


def norm_backward(upstream, normed, inverse, gain):
    scaled = upstream * gain
    expected = jnp.mean(scaled * normed, axis=-1, keepdims=True)
    return (scaled - normed * expected) * inverse


PEERS = LINE * LINE


def hops(offset):
    dz, dx = offset
    return 2 * min(dz, LINE - dz) + min(dx, LINE - dx)


OFFSETS = sorted(
    [(dz, dx) for dz in range(LINE) for dx in range(LINE)], key=lambda o: (o != (0, 0), o[0] > 0 and o[1] > 0, hops(o))
)
BACK = [OFFSETS.index(((LINE - dz) % LINE, (LINE - dx) % LINE)) for dz, dx in OFFSETS]
NEAR, FAR = (1, 7), (7, 16)
PARTS = ((0, 256), (256, 512), (512, 576))


def kernel(
    pl_hbm, pr_hbm, rl_hbm, rr_hbm, gain_hbm, q_hbm, c_hbm, len_hbm, mask_hbm, rew_hbm,
    o_pl, o_pr, o_rl, o_rr, o_gain,
    q_v, c_v, powers_v, grad_soft_v, stats, p_st, d_st, keys, normed, gathered, pl_v, pr_v, rl_v, rr_v, gain_v,
    len_s, mask_s, rew_s, acc, send_rows, recv_rows, gain_own, gain_a, gain_mid, gain_b,
    load_sem, g_send, g_recv, r_send, r_recv, a_send, a_recv, b_send, b_recv,
):
    rows, lat = c_v.shape
    wide = q_v.shape[1]
    rope = wide - lat
    local = rl_v.shape[0]
    own = pl_v.shape[0]
    count = keys.shape[0]

    me = lax.axis_index("resp")
    prompt = lax.axis_index("prompt")
    my_z, my_x = me // LINE, lax.rem(me, LINE)

    def shift(value, step):
        return lax.rem(value + step, LINE)

    def same_prompt(position):
        dz, dx = OFFSETS[position]
        return {"resp": shift(my_z, dz) * LINE + shift(my_x, dx)}

    def same_response(step):
        return {"prompt": lax.rem(prompt + step, PEERS)}

    small = [
        pltpu.make_async_copy(src, dst, load_sem.at[i])
        for i, (src, dst) in enumerate(
            ((pl_hbm, pl_v), (pr_hbm, pr_v), (rew_hbm, rew_s), (rl_hbm, rl_v), (rr_hbm, rr_v),
             (gain_hbm, gain_v), (len_hbm, len_s), (mask_hbm, mask_s))
        )
    ]
    for copy in small:
        copy.start()

    barrier = pltpu.get_barrier_semaphore()
    targets = [same_prompt(p) for p in range(NEAR[1] - 1, 0, -1)]
    targets += [same_response(s) for s in range(1, PEERS)]
    for target in targets:
        pl.semaphore_signal(barrier, inc=1, device_id=target, device_id_type=MESH)
    big = [
        pltpu.make_async_copy(q_hbm, q_v, load_sem.at[8]),
        pltpu.make_async_copy(c_hbm, c_v, load_sem.at[9]),
    ]
    for copy in big:
        copy.start()
    for copy in small:
        copy.wait()

    reward = jnp.full((own, rope), rew_s[0, 0], F32)
    high = reward.astype(BF16)
    rest = reward - high.astype(F32)
    mid = rest.astype(BF16)
    low = (rest - mid.astype(F32)).astype(BF16)
    lane = lax.broadcasted_iota(jnp.int32, (own, rope), 1)
    terms = jnp.where(
        lane == 0, high.astype(F32), jnp.where(lane == 1, mid.astype(F32), jnp.where(lane == 2, low.astype(F32), 0.0))
    )
    gathered[0, :, :lat] = pl_v[...]
    gathered[0, :, lat:] = jnp.concatenate([pr_v[...].astype(F32), terms], axis=1).astype(BF16)

    gain = gain_v[...]
    res_normed, res_inverse = normed_rows(rl_v[...])
    normed[:local, :] = res_normed
    keys[:local, :lat] = (res_normed * gain).astype(BF16)
    eye = (
        lax.broadcasted_iota(jnp.int32, (local, local), 0) == lax.broadcasted_iota(jnp.int32, (local, local), 1)
    ).astype(F32).astype(BF16)
    keys[:local, lat:] = lax.dot_general(eye, rr_v[...], NT, preferred_element_type=F32).astype(BF16)

    def place(first, last):
        lo, hi = local + first * own, local + last * own
        raw = gathered[first:last].reshape(hi - lo, lat + 2 * rope)
        rows_normed, rows_inverse = normed_rows(raw[:, :lat])
        normed[lo:hi, :] = rows_normed
        keys[lo:hi, :lat] = (rows_normed * gain).astype(BF16)
        keys[lo:hi, lat:] = raw[:, lat : lat + rope]
        return rows_normed, rows_inverse

    own_normed, own_inverse = place(0, 1)

    heads = rows // local
    per_block = BLK // heads
    column = lax.broadcasted_iota(jnp.int32, (1, BLK), 1)
    key_at = lax.broadcasted_iota(jnp.int32, (local, BLK), 0)
    token_in = lax.broadcasted_iota(jnp.int32, (local, BLK), 1) // heads
    length = len_s[0, 0]
    groups = tuple((local + a * own, local + b * own) for a, b in (NEAR, FAR))
    groups = ((0, groups[0][0]),) + groups

    def score(group):
        lo, hi = groups[group]

        def step(block, carry):
            at = pl.ds(pl.multiple_of(block * BLK, BLK), BLK)
            first = block * per_block
            scores = lax.dot_general(keys[lo:hi, :], q_v[at, :], NT, preferred_element_type=F32)
            grad_soft = lax.dot_general(keys[lo:hi, :lat], c_v[at, :], NT, preferred_element_type=F32)
            if group == 0:
                visible = key_at <= token_in + first
                scores = jnp.concatenate([jnp.where(visible, scores[:local], -jnp.inf), scores[local:]], axis=0)
            top = jnp.max(scores, axis=0, keepdims=True)
            powers = jnp.exp2((scores - top) * (SOFTMAX_SCALE * LOG2E))
            total = jnp.sum(powers, axis=0, keepdims=True)
            weighted = jnp.sum(powers * grad_soft, axis=0, keepdims=True)
            if group < 2:
                powers_v[lo:hi, at] = powers
                grad_soft_v[lo:hi, at] = grad_soft
                stats[3 * group : 3 * group + 1, at] = top
                stats[3 * group + 1 : 3 * group + 2, at] = total
                stats[3 * group + 2 : 3 * group + 3, at] = weighted
                return carry
            live = jnp.zeros((1, BLK), F32)
            for i in range(per_block):
                weight = jnp.where((first + i < length) & (mask_s[0, first + i] > 0), 1.0, 0.0)
                live = jnp.where((column >= i * heads) & (column < (i + 1) * heads), weight, live)
            tops = (stats[0:1, at], stats[3:4, at], top)
            maximum = jnp.maximum(jnp.maximum(tops[0], tops[1]), top)
            scales = [jnp.exp2((t - maximum) * (SOFTMAX_SCALE * LOG2E)) for t in tops]
            inverse = 1.0 / (scales[0] * stats[1:2, at] + scales[1] * stats[4:5, at] + scales[2] * total)
            expected = (scales[0] * stats[2:3, at] + scales[1] * stats[5:6, at] + scales[2] * weighted) * inverse
            for g, (a, b) in enumerate(groups):
                part = powers if g == 2 else powers_v[a:b, at]
                grads = grad_soft if g == 2 else grad_soft_v[a:b, at]
                soft = part * (scales[g] * inverse * live)
                p_st[a:b, at] = soft.astype(BF16)
                d_st[a:b, at] = (soft * (grads - expected)).astype(BF16)
            return carry

        lax.fori_loop(0, rows // BLK, step, 0, unroll=UNROLL)

    for copy in big:
        copy.wait()
    score(0)

    pl.semaphore_wait(barrier, len(targets))
    gathers = {}

    def pass_on(block, offset):
        (dz, dx), (ez, ex) = OFFSETS[block], offset
        there = OFFSETS.index(((dz - ez) % LINE, (dx - ex) % LINE))
        copy = pltpu.make_async_remote_copy(
            src_ref=gathered.at[block], dst_ref=gathered.at[there],
            send_sem=g_send.at[there], recv_sem=g_recv.at[there],
            device_id=same_prompt(OFFSETS.index(offset)), device_id_type=MESH,
        )
        copy.start()
        gathers[there] = copy

    for dz in (2, 1, 3):
        pass_on(0, (dz, 0))
    for dx in (2, 1, 3):
        pass_on(0, (0, dx))
    for dz in (1, 3, 2):
        block = OFFSETS.index((dz, 0))
        gathers[block].wait_recv()
        for dx in (2, 1, 3):
            pass_on(block, (0, dx))
    for dx in (1, 3, 2):
        gathers[OFFSETS.index((0, dx))].wait_recv()
    place(*NEAR)
    score(1)
    for p in range(*FAR):
        gathers[p].wait_recv()
    place(*FAR)
    score(2)
    for p in range(1, PEERS):
        gathers[p].wait_send()
    reward_sum = jnp.sum(gathered[:, :, lat:].astype(F32).reshape(PEERS * own, 2 * rope)[:, rope:]) / own
    factor = reward_sum / PEERS - rew_s[0, 0]

    def contract(stored, values, lo, hi):
        return jnp.dot(stored[...], values[:, lo:hi], preferred_element_type=F32)

    reduces = []
    for part, (lo, hi) in enumerate(PARTS):
        total = contract(d_st, q_v, lo, hi)
        if hi <= lat:
            total = total + contract(p_st, c_v, lo, hi) * (1.0 / SOFTMAX_SCALE)
        total = total * factor
        acc[:, lo:hi] = total
        if hi <= lat:
            gain_own[:, lo:hi] = jnp.sum(total * normed[:, lo:hi], axis=0, keepdims=True)
        if hi == lat:
            near = []
            for step in range(1, PEERS):
                copy = pltpu.make_async_remote_copy(
                    src_ref=gain_own, dst_ref=gain_a.at[BACK[step]],
                    send_sem=a_send.at[step], recv_sem=a_recv.at[BACK[step]],
                    device_id=same_prompt(step), device_id_type=MESH,
                )
                copy.start()
                near.append(copy)
        send_rows[:, :, lo:hi] = total[local:].astype(BF16).reshape(PEERS, own, hi - lo)
        for p in range(PEERS - 1, 0, -1):
            copy = pltpu.make_async_remote_copy(
                src_ref=send_rows.at[p, :, lo:hi], dst_ref=recv_rows.at[BACK[p], :, lo:hi],
                send_sem=r_send.at[part, p], recv_sem=r_recv.at[part, BACK[p]],
                device_id=same_prompt(p), device_id_type=MESH,
            )
            copy.start()
            reduces.append(copy)

    for copy in near:
        copy.wait()
    total_gain = gain_own[...]
    for step in range(1, PEERS):
        total_gain = total_gain + gain_a[step]
    gain_mid[...] = total_gain
    far = []
    for step in range(1, PEERS):
        copy = pltpu.make_async_remote_copy(
            src_ref=gain_mid, dst_ref=gain_b.at[step],
            send_sem=b_send.at[step], recv_sem=b_recv.at[step],
            device_id=same_response(step), device_id_type=MESH,
        )
        copy.start()
        far.append(copy)

    o_rl[...] = norm_backward(acc[:local, :lat], res_normed, res_inverse, gain)
    o_rr[...] = acc[:local, lat:].T
    for copy in reduces:
        copy.wait()
    total = acc[local : local + own, :]
    for p in range(1, PEERS):
        total = total + recv_rows[p].astype(F32)
    o_pl[...] = norm_backward(total[:, :lat], own_normed, own_inverse, gain)
    o_pr[...] = total[:, lat:]

    for copy in far:
        copy.wait()
    total_gain = gain_mid[...]
    for step in range(1, PEERS):
        total_gain = total_gain + gain_b[step]
    o_gain[...] = total_gain


def per_device(
    prefix_latent, prefix_rope, resp_latent, resp_rope, norm_gain, queries, cotangent, lengths, token_mask, rewards
):
    tokens, heads, wide = queries.shape[2:]
    lat = cotangent.shape[-1]
    rope = wide - lat
    own = prefix_latent.shape[1]
    rows = tokens * heads
    count = own * PEERS + tokens
    vmem, dma = pltpu.VMEM, pltpu.SemaphoreType.DMA
    shapes = ((own, lat), (own, rope), (tokens, lat), (rope, tokens), (1, lat))
    out = pl.pallas_call(
        kernel,
        out_shape=tuple(pltpu.VMEM(s, F32) for s in shapes),
        in_specs=[pl.BlockSpec(memory_space=pl.ANY)] * 10,
        out_specs=[pl.BlockSpec(memory_space=pltpu.VMEM)] * 5,
        scratch_shapes=[
            vmem((rows, wide), BF16),
            vmem((rows, lat), BF16),
            vmem((tokens + own * NEAR[1], rows), F32),
            vmem((tokens + own * NEAR[1], rows), F32),
            vmem((8, rows), F32),
            vmem((count, rows), BF16),
            vmem((count, rows), BF16),
            vmem((count, wide), BF16),
            vmem((count, lat), F32),
            vmem((PEERS, own, lat + 2 * rope), BF16),
            vmem((own, lat), BF16),
            vmem((own, rope), BF16),
            vmem((tokens, lat), BF16),
            vmem((rope, tokens), BF16),
            vmem((1, lat), F32),
            pltpu.SMEM((1, 1), jnp.int32),
            pltpu.SMEM((1, tokens), jnp.int32),
            pltpu.SMEM((1, 1), F32),
            vmem((count, wide), F32),
            vmem((PEERS, own, wide), BF16),
            vmem((PEERS, own, wide), BF16),
            vmem((1, lat), F32),
            vmem((PEERS, 1, lat), F32),
            vmem((1, lat), F32),
            vmem((PEERS, 1, lat), F32),
            dma((10,)),
            dma((PEERS,)),
            dma((PEERS,)),
            dma((len(PARTS), PEERS)),
            dma((len(PARTS), PEERS)),
            dma((PEERS,)),
            dma((PEERS,)),
            dma((PEERS,)),
            dma((PEERS,)),
        ],
        compiler_params=pltpu.CompilerParams(
            collective_id=0, has_side_effects=True, vmem_limit_bytes=56 * 2**20
        ),
        name="grpo_backward",
    )(
        prefix_latent[0],
        prefix_rope[0],
        resp_latent[0, 0],
        resp_rope[0, 0].T,
        norm_gain[None],
        queries.reshape(rows, wide),
        cotangent.reshape(rows, lat),
        lengths,
        token_mask[0],
        rewards,
    )
    out = [value * SOFTMAX_SCALE for value in out]
    return (out[0][None], out[1][None], out[2][None, None], out[3].T[None, None], out[4][0])


def solution(mesh):
    placed = (
        P("prompt", "resp", None),
        P("prompt", "resp", None),
        P("prompt", "resp", None, None),
        P("prompt", "resp", None, None),
        P(),
        P("prompt", "resp", None, None, None),
        P("prompt", "resp", None, None, None),
        P("prompt", "resp"),
        P("prompt", "resp", None),
        P("prompt", "resp"),
    )
    return jax.shard_map(
        per_device,
        mesh=mesh,
        in_specs=placed,
        out_specs=(
            P("prompt", "resp", None),
            P("prompt", "resp", None),
            P("prompt", "resp", None, None),
            P("prompt", "resp", None, None),
            P(),
        ),
        check_vma=False,
    )
```

```python
import jax
import jax.numpy as jnp
from jax import lax
from jax.experimental import pallas as pl
from jax.experimental.pallas import tpu as pltpu
from jax.sharding import PartitionSpec as P

SOFTMAX_SCALE = 192.0 ** (-0.5)
LOG2E = 1.4426950408889634
NORM_EPSILON = 1e-06
NT = (((1,), (1,)), ((), ()))
LINE = 4
BLK = 512
UNROLL = 5
MESH = pl.DeviceIdType.MESH
F32, BF16 = jnp.float32, jnp.bfloat16


def normed_rows(raw):
    values = raw.astype(F32)
    inverse = lax.rsqrt(jnp.mean(values * values, axis=-1, keepdims=True) + NORM_EPSILON)
    return values * inverse, inverse


def norm_backward(upstream, normed, inverse, gain):
    scaled = upstream * gain
    expected = jnp.mean(scaled * normed, axis=-1, keepdims=True)
    return (scaled - normed * expected) * inverse


PEERS = LINE * LINE


def hops(offset):
    dz, dx = offset
    return 2 * min(dz, LINE - dz) + min(dx, LINE - dx)


OFFSETS = sorted(
    [(dz, dx) for dz in range(LINE) for dx in range(LINE)], key=lambda o: (o != (0, 0), o[0] > 0 and o[1] > 0, hops(o))
)
BACK = [OFFSETS.index(((LINE - dz) % LINE, (LINE - dx) % LINE)) for dz, dx in OFFSETS]
NEAR, FAR = (1, 7), (7, 16)
PARTS = ((0, 256), (256, 512), (512, 576))


def kernel(
    pl_hbm, pr_hbm, rl_hbm, rr_hbm, gain_hbm, q_hbm, c_hbm, len_hbm, mask_hbm, rew_hbm,
    o_pl, o_pr, o_rl, o_rr, o_gain,
    q_v, c_v, powers_v, grad_soft_v, stats, p_st, d_st, keys, normed, gathered, pl_v, pr_v, rl_v, rr_v, gain_v,
    len_s, mask_s, rew_s, acc, send_x, recv_x, send_z, recv_z, gain_own, gain_a, gain_mid, gain_b,
    token, load_sem, g_send, g_recv, x_send, x_recv, z_send, z_recv, a_send, a_recv, b_send, b_recv,
):
    rows, lat = c_v.shape
    wide = q_v.shape[1]
    rope = wide - lat
    local = rl_v.shape[0]
    own = pl_v.shape[0]
    count = keys.shape[0]

    me = lax.axis_index("resp")
    prompt = lax.axis_index("prompt")
    my_z, my_x = me // LINE, lax.rem(me, LINE)

    def shift(value, step):
        return lax.rem(value + step, LINE)

    def same_prompt(position):
        dz, dx = OFFSETS[position]
        return {"resp": shift(my_z, dz) * LINE + shift(my_x, dx)}

    def same_response(step):
        return {"prompt": lax.rem(prompt + step, PEERS)}

    my_y, my_low, my_core = prompt // LINE, lax.rem(prompt, LINE) // 2, lax.rem(prompt, 2)

    def near_prompt(dy, dlow, dcore):
        low, core = lax.rem(my_low + dlow, 2), lax.rem(my_core + dcore, 2)
        return {"prompt": shift(my_y, dy) * LINE + low * 2 + core}

    small = [
        pltpu.make_async_copy(src, dst, load_sem.at[i])
        for i, (src, dst) in enumerate(
            ((pl_hbm, pl_v), (pr_hbm, pr_v), (rew_hbm, rew_s), (rl_hbm, rl_v), (rr_hbm, rr_v),
             (gain_hbm, gain_v), (len_hbm, len_s), (mask_hbm, mask_s))
        )
    ]
    for copy in small:
        copy.start()

    barrier = pltpu.get_barrier_semaphore()
    targets = [same_prompt(OFFSETS.index(o)) for o in ((1, 0), (3, 0), (0, 2), (0, 1), (0, 3))]
    targets += [
        near_prompt(dy, dlow, dcore)
        for dy in (2, 1, 3, 0) for dlow in (1, 0) for dcore in (0, 1)
        if (dy, dlow, dcore) != (0, 0, 0) and (dy, dlow) != (2, 1)
    ]
    for target in targets:
        pl.semaphore_signal(barrier, inc=1, device_id=target, device_id_type=MESH)
    halves = tuple(pl.ds(start, rows // 2) for start in (0, rows // 2))
    big = [
        pltpu.make_async_copy(src.at[half], dst.at[half], load_sem.at[8 + 2 * i + j])
        for i, half in enumerate(halves) for j, (src, dst) in enumerate(((q_hbm, q_v), (c_hbm, c_v)))
    ]
    for copy in big:
        copy.start()
    for copy in small:
        copy.wait()

    reward = jnp.full((own, rope), rew_s[0, 0], F32)
    high = reward.astype(BF16)
    rest = reward - high.astype(F32)
    mid = rest.astype(BF16)
    low = (rest - mid.astype(F32)).astype(BF16)
    lane = lax.broadcasted_iota(jnp.int32, (own, rope), 1)
    terms = jnp.where(
        lane == 0, high.astype(F32), jnp.where(lane == 1, mid.astype(F32), jnp.where(lane == 2, low.astype(F32), 0.0))
    )
    gathered[0, :, :lat] = pl_v[...]
    gathered[0, :, lat:] = jnp.concatenate([pr_v[...].astype(F32), terms], axis=1).astype(BF16)

    gain = gain_v[...]
    res_normed, res_inverse = normed_rows(rl_v[...])
    normed[:local, :] = res_normed
    keys[:local, :lat] = (res_normed * gain).astype(BF16)
    eye = (
        lax.broadcasted_iota(jnp.int32, (local, local), 0) == lax.broadcasted_iota(jnp.int32, (local, local), 1)
    ).astype(F32).astype(BF16)
    keys[:local, lat:] = lax.dot_general(eye, rr_v[...], NT, preferred_element_type=F32).astype(BF16)

    def place(first, last):
        lo, hi = local + first * own, local + last * own
        raw = gathered[first:last].reshape(hi - lo, lat + 2 * rope)
        rows_normed, rows_inverse = normed_rows(raw[:, :lat])
        normed[lo:hi, :] = rows_normed
        keys[lo:hi, :lat] = (rows_normed * gain).astype(BF16)
        keys[lo:hi, lat:] = raw[:, lat : lat + rope]
        return rows_normed, rows_inverse

    own_normed, own_inverse = place(0, 1)

    heads = rows // local
    per_block = BLK // heads
    column = lax.broadcasted_iota(jnp.int32, (1, BLK), 1)
    key_at = lax.broadcasted_iota(jnp.int32, (local, BLK), 0)
    token_in = lax.broadcasted_iota(jnp.int32, (local, BLK), 1) // heads
    length = len_s[0, 0]
    groups = tuple((local + a * own, local + b * own) for a, b in (NEAR, FAR))
    groups = ((0, groups[0][0]),) + groups

    def score(group, first_block, last_block):
        lo, hi = groups[group]

        def step(block, carry):
            at = pl.ds(pl.multiple_of(block * BLK, BLK), BLK)
            first = block * per_block
            scores = lax.dot_general(keys[lo:hi, :], q_v[at, :], NT, preferred_element_type=F32)
            grad_soft = lax.dot_general(keys[lo:hi, :lat], c_v[at, :], NT, preferred_element_type=F32)
            if group == 0:
                visible = key_at <= token_in + first
                scores = jnp.concatenate([jnp.where(visible, scores[:local], -jnp.inf), scores[local:]], axis=0)
            top = jnp.max(scores, axis=0, keepdims=True)
            powers = jnp.exp2((scores - top) * (SOFTMAX_SCALE * LOG2E))
            total = jnp.sum(powers, axis=0, keepdims=True)
            weighted = jnp.sum(powers * grad_soft, axis=0, keepdims=True)
            if group < 2:
                powers_v[lo:hi, at] = powers
                grad_soft_v[lo:hi, at] = grad_soft
                stats[3 * group : 3 * group + 1, at] = top
                stats[3 * group + 1 : 3 * group + 2, at] = total
                stats[3 * group + 2 : 3 * group + 3, at] = weighted
                return carry
            live = jnp.zeros((1, BLK), F32)
            for i in range(per_block):
                weight = jnp.where((first + i < length) & (mask_s[0, first + i] > 0), 1.0, 0.0)
                live = jnp.where((column >= i * heads) & (column < (i + 1) * heads), weight, live)
            tops = (stats[0:1, at], stats[3:4, at], top)
            maximum = jnp.maximum(jnp.maximum(tops[0], tops[1]), top)
            scales = [jnp.exp2((t - maximum) * (SOFTMAX_SCALE * LOG2E)) for t in tops]
            inverse = 1.0 / (scales[0] * stats[1:2, at] + scales[1] * stats[4:5, at] + scales[2] * total)
            expected = (scales[0] * stats[2:3, at] + scales[1] * stats[5:6, at] + scales[2] * weighted) * inverse
            for g, (a, b) in enumerate(groups):
                part = powers if g == 2 else powers_v[a:b, at]
                grads = grad_soft if g == 2 else grad_soft_v[a:b, at]
                soft = part * (scales[g] * inverse * live)
                p_st[a:b, at] = soft.astype(BF16)
                d_st[a:b, at] = (soft * (grads - expected)).astype(BF16)
            return carry

        lax.fori_loop(first_block, last_block, step, 0, unroll=UNROLL)

    pl.semaphore_wait(barrier, len(targets))
    gathers = {}

    def pass_on(block, offset):
        (dz, dx), (ez, ex) = OFFSETS[block], offset
        there = OFFSETS.index(((dz - ez) % LINE, (dx - ex) % LINE))
        copy = pltpu.make_async_remote_copy(
            src_ref=gathered.at[block], dst_ref=gathered.at[there],
            send_sem=g_send.at[there], recv_sem=g_recv.at[there],
            device_id=same_prompt(OFFSETS.index(offset)), device_id_type=MESH,
        )
        copy.start()
        gathers[there] = copy

    half = rows // BLK // 2
    for dz in (1, 3):
        pass_on(0, (dz, 0))
    for dx in (2, 1, 3):
        pass_on(0, (0, dx))
    pl.semaphore_signal(token, inc=1, device_id=near_prompt(0, 1, 0), device_id_type=MESH)
    for copy in big[:2]:
        copy.wait()
    score(0, 0, half)
    for dz in (3, 1):
        block = OFFSETS.index((dz, 0))
        gathers[block].wait_recv()
        if dz == 3:
            pass_on(block, (1, 0))
        for dx in (2, 1, 3):
            pass_on(block, (0, dx))
    for copy in big[2:]:
        copy.wait()
    score(0, half, 2 * half)
    block = OFFSETS.index((2, 0))
    gathers[block].wait_recv()
    for dx in (2, 1, 3):
        pass_on(block, (0, dx))
    for dx in (1, 3, 2):
        gathers[OFFSETS.index((0, dx))].wait_recv()
    place(*NEAR)
    score(1, 0, 2 * half)
    for p in range(*FAR):
        gathers[p].wait_recv()
    place(*FAR)
    score(2, 0, 2 * half)
    pl.semaphore_wait(token, 1)
    for p in range(1, PEERS):
        gathers[p].wait_send()
    reward_sum = jnp.sum(gathered[:, :, lat:].astype(F32).reshape(PEERS * own, 2 * rope)[:, rope:]) / own
    factor = reward_sum / PEERS - rew_s[0, 0]

    def contract(stored, values, lo, hi):
        return jnp.dot(stored[...], values[:, lo:hi], preferred_element_type=F32)

    along_x = []
    order = [[local + own * OFFSETS.index((dz, dx)) for dz in range(LINE)] for dx in range(LINE)]
    for part, (lo, hi) in enumerate(PARTS):
        total = contract(d_st, q_v, lo, hi)
        if hi <= lat:
            total = total + contract(p_st, c_v, lo, hi) * (1.0 / SOFTMAX_SCALE)
        total = total * factor
        acc[:, lo:hi] = total
        if hi <= lat:
            gain_own[:, lo:hi] = jnp.sum(total * normed[:, lo:hi], axis=0, keepdims=True)
        if hi == lat:
            near = []
            for step in range(1, PEERS):
                copy = pltpu.make_async_remote_copy(
                    src_ref=gain_own, dst_ref=gain_a.at[BACK[step]],
                    send_sem=a_send.at[step], recv_sem=a_recv.at[BACK[step]],
                    device_id=same_prompt(step), device_id_type=MESH,
                )
                copy.start()
                near.append(copy)
        for dx in range(1, LINE):
            for dz in range(LINE):
                at = order[dx][dz]
                send_x[dx, dz, :, lo:hi] = total[at : at + own].astype(BF16)
        started = []
        for dx in (2, 1, 3):
            copy = pltpu.make_async_remote_copy(
                src_ref=send_x.at[dx, :, :, lo:hi], dst_ref=recv_x.at[dx, :, :, lo:hi],
                send_sem=x_send.at[part, dx], recv_sem=x_recv.at[part, dx],
                device_id=same_prompt(OFFSETS.index((0, dx))), device_id_type=MESH,
            )
            copy.start()
            started.append(copy)
        along_x.append(started)

    along_z = []
    for part, (lo, hi) in enumerate(PARTS):
        for copy in along_x[part]:
            copy.wait()
        for dz in range(LINE):
            at = order[0][dz]
            total = acc[at : at + own, lo:hi]
            for dx in range(1, LINE):
                total = total + recv_x[dx, dz, :, lo:hi].astype(F32)
            if dz == 0:
                acc[at : at + own, lo:hi] = total
            else:
                send_z[dz, :, lo:hi] = total.astype(BF16)
        for dz in (2, 1, 3):
            copy = pltpu.make_async_remote_copy(
                src_ref=send_z.at[dz, :, lo:hi], dst_ref=recv_z.at[dz, :, lo:hi],
                send_sem=z_send.at[part, dz], recv_sem=z_recv.at[part, dz],
                device_id=same_prompt(OFFSETS.index((dz, 0))), device_id_type=MESH,
            )
            copy.start()
            along_z.append(copy)

    for copy in near:
        copy.wait()
    total_gain = gain_own[...]
    for step in range(1, PEERS):
        total_gain = total_gain + gain_a[step]
    gain_mid[...] = total_gain
    far = []
    for step in range(1, PEERS):
        copy = pltpu.make_async_remote_copy(
            src_ref=gain_mid, dst_ref=gain_b.at[step],
            send_sem=b_send.at[step], recv_sem=b_recv.at[step],
            device_id=same_response(step), device_id_type=MESH,
        )
        copy.start()
        far.append(copy)

    o_rl[...] = norm_backward(acc[:local, :lat], res_normed, res_inverse, gain)
    o_rr[...] = acc[:local, lat:].T
    for copy in along_z:
        copy.wait()
    total = acc[local : local + own, :]
    for dz in range(1, LINE):
        total = total + recv_z[dz].astype(F32)
    o_pl[...] = norm_backward(total[:, :lat], own_normed, own_inverse, gain)
    o_pr[...] = total[:, lat:]

    for copy in far:
        copy.wait()
    total_gain = gain_mid[...]
    for step in range(1, PEERS):
        total_gain = total_gain + gain_b[step]
    o_gain[...] = total_gain


def per_device(
    prefix_latent, prefix_rope, resp_latent, resp_rope, norm_gain, queries, cotangent, lengths, token_mask, rewards
):
    tokens, heads, wide = queries.shape[2:]
    lat = cotangent.shape[-1]
    rope = wide - lat
    own = prefix_latent.shape[1]
    rows = tokens * heads
    count = own * PEERS + tokens
    vmem, dma = pltpu.VMEM, pltpu.SemaphoreType.DMA
    shapes = ((own, lat), (own, rope), (tokens, lat), (rope, tokens), (1, lat))
    out = pl.pallas_call(
        kernel,
        out_shape=tuple(pltpu.VMEM(s, F32) for s in shapes),
        in_specs=[pl.BlockSpec(memory_space=pl.ANY)] * 10,
        out_specs=[pl.BlockSpec(memory_space=pltpu.VMEM)] * 5,
        scratch_shapes=[
            vmem((rows, wide), BF16),
            vmem((rows, lat), BF16),
            vmem((tokens + own * NEAR[1], rows), F32),
            vmem((tokens + own * NEAR[1], rows), F32),
            vmem((8, rows), F32),
            vmem((count, rows), BF16),
            vmem((count, rows), BF16),
            vmem((count, wide), BF16),
            vmem((count, lat), F32),
            vmem((PEERS, own, lat + 2 * rope), BF16),
            vmem((own, lat), BF16),
            vmem((own, rope), BF16),
            vmem((tokens, lat), BF16),
            vmem((rope, tokens), BF16),
            vmem((1, lat), F32),
            pltpu.SMEM((1, 1), jnp.int32),
            pltpu.SMEM((1, tokens), jnp.int32),
            pltpu.SMEM((1, 1), F32),
            vmem((count, wide), F32),
            vmem((LINE, LINE, own, wide), BF16),
            vmem((LINE, LINE, own, wide), BF16),
            vmem((LINE, own, wide), BF16),
            vmem((LINE, own, wide), BF16),
            vmem((1, lat), F32),
            vmem((PEERS, 1, lat), F32),
            vmem((1, lat), F32),
            vmem((PEERS, 1, lat), F32),
            pltpu.SemaphoreType.REGULAR,
            dma((12,)),
            dma((PEERS,)),
            dma((PEERS,)),
            dma((len(PARTS), LINE)),
            dma((len(PARTS), LINE)),
            dma((len(PARTS), LINE)),
            dma((len(PARTS), LINE)),
            dma((PEERS,)),
            dma((PEERS,)),
            dma((PEERS,)),
            dma((PEERS,)),
        ],
        compiler_params=pltpu.CompilerParams(
            collective_id=0, has_side_effects=True, vmem_limit_bytes=56 * 2**20
        ),
        name="grpo_backward",
    )(
        prefix_latent[0],
        prefix_rope[0],
        resp_latent[0, 0],
        resp_rope[0, 0].T,
        norm_gain[None],
        queries.reshape(rows, wide),
        cotangent.reshape(rows, lat),
        lengths,
        token_mask[0],
        rewards,
    )
    out = [value * SOFTMAX_SCALE for value in out]
    return (out[0][None], out[1][None], out[2][None, None], out[3].T[None, None], out[4][0])


def solution(mesh):
    placed = (
        P("prompt", "resp", None),
        P("prompt", "resp", None),
        P("prompt", "resp", None, None),
        P("prompt", "resp", None, None),
        P(),
        P("prompt", "resp", None, None, None),
        P("prompt", "resp", None, None, None),
        P("prompt", "resp"),
        P("prompt", "resp", None),
        P("prompt", "resp"),
    )
    return jax.shard_map(
        per_device,
        mesh=mesh,
        in_specs=placed,
        out_specs=(
            P("prompt", "resp", None),
            P("prompt", "resp", None),
            P("prompt", "resp", None, None),
            P("prompt", "resp", None, None),
            P(),
        ),
        check_vma=False,
    )
```

```python
import jax
import jax.numpy as jnp
from jax import lax
from jax.experimental import pallas as pl
from jax.experimental.pallas import tpu as pltpu
from jax.sharding import PartitionSpec as P

SOFTMAX_SCALE = 192.0 ** (-0.5)
LOG2E = 1.4426950408889634
NORM_EPSILON = 1e-06
NT = (((1,), (1,)), ((), ()))
LINE = 4
BLK = 512
UNROLL = 5
MESH = pl.DeviceIdType.MESH
F32, BF16 = jnp.float32, jnp.bfloat16


def normed_rows(raw):
    values = raw.astype(F32)
    inverse = lax.rsqrt(jnp.mean(values * values, axis=-1, keepdims=True) + NORM_EPSILON)
    return values * inverse, inverse


def norm_backward(upstream, normed, inverse, gain):
    scaled = upstream * gain
    expected = jnp.mean(scaled * normed, axis=-1, keepdims=True)
    return (scaled - normed * expected) * inverse


PEERS = LINE * LINE


def hops(offset):
    dz, dx = offset
    return 2 * min(dz, LINE - dz) + min(dx, LINE - dx)


OFFSETS = sorted(
    [(dz, dx) for dz in range(LINE) for dx in range(LINE)], key=lambda o: (o != (0, 0), o[0] > 0 and o[1] > 0, hops(o))
)
BACK = [OFFSETS.index(((LINE - dz) % LINE, (LINE - dx) % LINE)) for dz, dx in OFFSETS]
NEAR, FAR = (1, 7), (7, 16)
PARTS = ((0, 256), (256, 512), (512, 576))


def kernel(
    pl_hbm, pr_hbm, rl_hbm, rr_hbm, gain_hbm, q_hbm, c_hbm, len_hbm, mask_hbm, rew_hbm,
    o_pl, o_pr, o_rl, o_rr, o_gain,
    q_v, c_v, powers_v, grad_soft_v, stats, p_st, d_st, keys, normed, gathered, pl_v, pr_v, rl_v, rr_v, gain_v,
    len_s, mask_s, rew_s, acc, send_x, recv_x, send_z, recv_z, gain_own, gain_a, gain_mid, gain_b,
    token, load_sem, g_send, g_recv, x_send, x_recv, z_send, z_recv, a_send, a_recv, b_send, b_recv,
):
    rows, lat = c_v.shape
    wide = q_v.shape[1]
    rope = wide - lat
    local = rl_v.shape[0]
    own = pl_v.shape[0]
    count = keys.shape[0]

    me = lax.axis_index("resp")
    prompt = lax.axis_index("prompt")
    my_z, my_x = me // LINE, lax.rem(me, LINE)

    def shift(value, step):
        return lax.rem(value + step, LINE)

    def same_prompt(position):
        dz, dx = OFFSETS[position]
        return {"resp": shift(my_z, dz) * LINE + shift(my_x, dx)}

    def same_plane(step):
        return {
            "prompt": shift(prompt // LINE, step // LINE) * LINE + lax.rem(prompt, LINE),
            "resp": my_z * LINE + shift(my_x, step % LINE),
        }

    def same_column(step):
        return {
            "prompt": prompt // LINE * LINE + shift(lax.rem(prompt, LINE), step // LINE),
            "resp": shift(my_z, step % LINE) * LINE + my_x,
        }

    my_y, my_low, my_core = prompt // LINE, lax.rem(prompt, LINE) // 2, lax.rem(prompt, 2)

    def near_prompt(dy, dlow, dcore):
        low, core = lax.rem(my_low + dlow, 2), lax.rem(my_core + dcore, 2)
        return {"prompt": shift(my_y, dy) * LINE + low * 2 + core}

    small = [
        pltpu.make_async_copy(src, dst, load_sem.at[i])
        for i, (src, dst) in enumerate(
            ((pl_hbm, pl_v), (pr_hbm, pr_v), (rew_hbm, rew_s), (rl_hbm, rl_v), (rr_hbm, rr_v),
             (gain_hbm, gain_v), (len_hbm, len_s), (mask_hbm, mask_s))
        )
    ]
    for copy in small:
        copy.start()

    barrier = pltpu.get_barrier_semaphore()
    targets = [same_prompt(OFFSETS.index(o)) for o in ((1, 0), (3, 0), (0, 2), (0, 1), (0, 3))]
    targets += [
        near_prompt(dy, dlow, dcore)
        for dy in (2, 1, 3, 0) for dlow in (1, 0) for dcore in (0, 1)
        if (dy, dlow, dcore) != (0, 0, 0) and (dy, dlow) != (2, 1)
    ]
    for target in targets:
        pl.semaphore_signal(barrier, inc=1, device_id=target, device_id_type=MESH)
    halves = tuple(pl.ds(start, rows // 2) for start in (0, rows // 2))
    big = [
        pltpu.make_async_copy(src.at[half], dst.at[half], load_sem.at[8 + 2 * i + j])
        for i, half in enumerate(halves) for j, (src, dst) in enumerate(((q_hbm, q_v), (c_hbm, c_v)))
    ]
    for copy in big:
        copy.start()
    for copy in small[:3]:
        copy.wait()

    reward = jnp.full((own, rope), rew_s[0, 0], F32)
    high = reward.astype(BF16)
    rest = reward - high.astype(F32)
    mid = rest.astype(BF16)
    low = (rest - mid.astype(F32)).astype(BF16)
    lane = lax.broadcasted_iota(jnp.int32, (own, rope), 1)
    terms = jnp.where(
        lane == 0, high.astype(F32), jnp.where(lane == 1, mid.astype(F32), jnp.where(lane == 2, low.astype(F32), 0.0))
    )
    gathered[0, :, :lat] = pl_v[...]
    gathered[0, :, lat:] = jnp.concatenate([pr_v[...].astype(F32), terms], axis=1).astype(BF16)

    pl.semaphore_wait(barrier, len(targets))
    gathers = {}

    def pass_on(block, offset):
        (dz, dx), (ez, ex) = OFFSETS[block], offset
        there = OFFSETS.index(((dz - ez) % LINE, (dx - ex) % LINE))
        copy = pltpu.make_async_remote_copy(
            src_ref=gathered.at[block], dst_ref=gathered.at[there],
            send_sem=g_send.at[there], recv_sem=g_recv.at[there],
            device_id=same_prompt(OFFSETS.index(offset)), device_id_type=MESH,
        )
        copy.start()
        gathers[there] = copy

    for dz in (1, 3):
        pass_on(0, (dz, 0))
    for dx in (2, 1, 3):
        pass_on(0, (0, dx))
    for copy in small[3:]:
        copy.wait()

    gain = gain_v[...]
    res_normed, res_inverse = normed_rows(rl_v[...])
    normed[:local, :] = res_normed
    keys[:local, :lat] = (res_normed * gain).astype(BF16)
    eye = (
        lax.broadcasted_iota(jnp.int32, (local, local), 0) == lax.broadcasted_iota(jnp.int32, (local, local), 1)
    ).astype(F32).astype(BF16)
    keys[:local, lat:] = lax.dot_general(eye, rr_v[...], NT, preferred_element_type=F32).astype(BF16)

    def place(first, last):
        lo, hi = local + first * own, local + last * own
        raw = gathered[first:last].reshape(hi - lo, lat + 2 * rope)
        rows_normed, rows_inverse = normed_rows(raw[:, :lat])
        normed[lo:hi, :] = rows_normed
        keys[lo:hi, :lat] = (rows_normed * gain).astype(BF16)
        keys[lo:hi, lat:] = raw[:, lat : lat + rope]
        return rows_normed, rows_inverse

    own_normed, own_inverse = place(0, 1)

    heads = rows // local
    half = rows // BLK // 2
    per_block = BLK // heads
    column = lax.broadcasted_iota(jnp.int32, (1, BLK), 1)
    key_at = lax.broadcasted_iota(jnp.int32, (local, BLK), 0)
    token_in = lax.broadcasted_iota(jnp.int32, (local, BLK), 1) // heads
    length = len_s[0, 0]
    groups = tuple((local + a * own, local + b * own) for a, b in (NEAR, FAR))
    groups = ((0, groups[0][0]),) + groups

    def score(group, first_block, last_block):
        lo, hi = groups[group]

        def step(block, carry):
            at = pl.ds(pl.multiple_of(block * BLK, BLK), BLK)
            first = block * per_block
            scores = lax.dot_general(keys[lo:hi, :], q_v[at, :], NT, preferred_element_type=F32)
            grad_soft = lax.dot_general(keys[lo:hi, :lat], c_v[at, :], NT, preferred_element_type=F32)
            if group == 0:
                visible = key_at <= token_in + first
                scores = jnp.concatenate([jnp.where(visible, scores[:local], -jnp.inf), scores[local:]], axis=0)
            top = jnp.max(scores, axis=0, keepdims=True)
            powers = jnp.exp2((scores - top) * (SOFTMAX_SCALE * LOG2E))
            total = jnp.sum(powers, axis=0, keepdims=True)
            weighted = jnp.sum(powers * grad_soft, axis=0, keepdims=True)
            if group < 2:
                powers_v[lo:hi, at] = powers
                grad_soft_v[lo:hi, at] = grad_soft
                stats[3 * group : 3 * group + 1, at] = top
                stats[3 * group + 1 : 3 * group + 2, at] = total
                stats[3 * group + 2 : 3 * group + 3, at] = weighted
                return carry
            live = jnp.zeros((1, BLK), F32)
            for i in range(per_block):
                weight = jnp.where((first + i < length) & (mask_s[0, first + i] > 0), 1.0, 0.0)
                live = jnp.where((column >= i * heads) & (column < (i + 1) * heads), weight, live)
            tops = (stats[0:1, at], stats[3:4, at], top)
            maximum = jnp.maximum(jnp.maximum(tops[0], tops[1]), top)
            scales = [jnp.exp2((t - maximum) * (SOFTMAX_SCALE * LOG2E)) for t in tops]
            inverse = 1.0 / (scales[0] * stats[1:2, at] + scales[1] * stats[4:5, at] + scales[2] * total)
            expected = (scales[0] * stats[2:3, at] + scales[1] * stats[5:6, at] + scales[2] * weighted) * inverse
            for g, (a, b) in enumerate(groups):
                part = powers if g == 2 else powers_v[a:b, at]
                grads = grad_soft if g == 2 else grad_soft_v[a:b, at]
                soft = part * (scales[g] * inverse * live)
                p_st[a:b, at] = soft.astype(BF16)
                d_st[a:b, at] = (soft * (grads - expected)).astype(BF16)
            return carry

        lax.fori_loop(first_block, last_block, step, 0, unroll=UNROLL)

    for copy in big[:2]:
        copy.wait()
    score(0, 0, half)
    for dz in (3, 1):
        block = OFFSETS.index((dz, 0))
        gathers[block].wait_recv()
        if dz == 3:
            pass_on(block, (1, 0))
        for dx in (2, 1, 3):
            pass_on(block, (0, dx))
    for copy in big[2:]:
        copy.wait()
    score(0, half, 2 * half)
    block = OFFSETS.index((2, 0))
    gathers[block].wait_recv()
    for dx in (2, 1, 3):
        pass_on(block, (0, dx))
    for dx in (1, 3, 2):
        gathers[OFFSETS.index((0, dx))].wait_recv()
    place(*NEAR)
    score(1, 0, 2 * half)
    for p in range(*FAR):
        gathers[p].wait_recv()
    place(*FAR)
    for step in range(LINE, PEERS, LINE):
        pl.semaphore_signal(token, inc=1, device_id=same_plane(step), device_id_type=MESH)
        pl.semaphore_signal(token, inc=1, device_id=same_column(step), device_id_type=MESH)
    score(2, 0, 2 * half)
    for p in range(1, PEERS):
        gathers[p].wait_send()
    reward_rows = jnp.sum(gathered[:, :, lat:].astype(F32).reshape(PEERS * own, 2 * rope)[:, rope:], axis=0, keepdims=True)
    factor = jnp.sum(reward_rows, axis=1, keepdims=True) / (own * PEERS) - rew_s[0, 0]

    def contract(stored, values, lo, hi):
        return jnp.dot(stored[...], values[:, lo:hi], preferred_element_type=F32)

    along_x = []
    order = [[local + own * OFFSETS.index((dz, dx)) for dz in range(LINE)] for dx in range(LINE)]
    for part, (lo, hi) in enumerate(PARTS):
        total = contract(d_st, q_v, lo, hi)
        if hi <= lat:
            total = total + contract(p_st, c_v, lo, hi) * (1.0 / SOFTMAX_SCALE)
        total = total * factor
        acc[:, lo:hi] = total
        if hi <= lat:
            gain_own[:, lo:hi] = jnp.sum(total * normed[:, lo:hi], axis=0, keepdims=True)
        if hi == lat:
            pl.semaphore_wait(token, 2 * (LINE - 1))
            near = []
            for step in range(1, PEERS):
                copy = pltpu.make_async_remote_copy(
                    src_ref=gain_own, dst_ref=gain_a.at[step],
                    send_sem=a_send.at[step], recv_sem=a_recv.at[step],
                    device_id=same_plane(step), device_id_type=MESH,
                )
                copy.start()
                near.append(copy)
        for dx in range(1, LINE):
            for dz in range(LINE):
                at = order[dx][dz]
                send_x[dx, dz, :, lo:hi] = total[at : at + own].astype(BF16)
        started = []
        for dx in (2, 1, 3):
            copy = pltpu.make_async_remote_copy(
                src_ref=send_x.at[dx, :, :, lo:hi], dst_ref=recv_x.at[dx, :, :, lo:hi],
                send_sem=x_send.at[part, dx], recv_sem=x_recv.at[part, dx],
                device_id=same_prompt(OFFSETS.index((0, dx))), device_id_type=MESH,
            )
            copy.start()
            started.append(copy)
        along_x.append(started)

    along_z = []
    for part, (lo, hi) in enumerate(PARTS):
        if part == len(PARTS) - 1:
            for copy in near:
                copy.wait()
            total_gain = gain_own[...]
            for step in range(1, PEERS):
                total_gain = total_gain + gain_a[step]
            gain_mid[...] = total_gain
            far = []
            for step in range(1, PEERS):
                copy = pltpu.make_async_remote_copy(
                    src_ref=gain_mid, dst_ref=gain_b.at[step],
                    send_sem=b_send.at[step], recv_sem=b_recv.at[step],
                    device_id=same_column(step), device_id_type=MESH,
                )
                copy.start()
                far.append(copy)
        for copy in along_x[part]:
            copy.wait()
        for dz in range(LINE):
            at = order[0][dz]
            total = acc[at : at + own, lo:hi]
            for dx in range(1, LINE):
                total = total + recv_x[dx, dz, :, lo:hi].astype(F32)
            if dz == 0:
                acc[at : at + own, lo:hi] = total
            else:
                send_z[dz, :, lo:hi] = total.astype(BF16)
        for dz in (2, 1, 3):
            copy = pltpu.make_async_remote_copy(
                src_ref=send_z.at[dz, :, lo:hi], dst_ref=recv_z.at[dz, :, lo:hi],
                send_sem=z_send.at[part, dz], recv_sem=z_recv.at[part, dz],
                device_id=same_prompt(OFFSETS.index((dz, 0))), device_id_type=MESH,
            )
            copy.start()
            along_z.append(copy)

    o_rl[...] = norm_backward(acc[:local, :lat], res_normed, res_inverse, gain)
    o_rr[...] = acc[:local, lat:].T
    for copy in along_z:
        copy.wait()
    total = acc[local : local + own, :]
    for dz in range(1, LINE):
        total = total + recv_z[dz].astype(F32)
    o_pl[...] = norm_backward(total[:, :lat], own_normed, own_inverse, gain)
    o_pr[...] = total[:, lat:]

    for copy in far:
        copy.wait()
    total_gain = gain_mid[...]
    for step in range(1, PEERS):
        total_gain = total_gain + gain_b[step]
    o_gain[...] = total_gain


def per_device(
    prefix_latent, prefix_rope, resp_latent, resp_rope, norm_gain, queries, cotangent, lengths, token_mask, rewards
):
    tokens, heads, wide = queries.shape[2:]
    lat = cotangent.shape[-1]
    rope = wide - lat
    own = prefix_latent.shape[1]
    rows = tokens * heads
    count = own * PEERS + tokens
    vmem, dma = pltpu.VMEM, pltpu.SemaphoreType.DMA
    shapes = ((own, lat), (own, rope), (tokens, lat), (rope, tokens), (1, lat))
    out = pl.pallas_call(
        kernel,
        out_shape=tuple(pltpu.VMEM(s, F32) for s in shapes),
        in_specs=[pl.BlockSpec(memory_space=pltpu.HBM)] * 10,
        out_specs=[pl.BlockSpec(memory_space=pltpu.VMEM)] * 5,
        scratch_shapes=[
            vmem((rows, wide), BF16),
            vmem((rows, lat), BF16),
            vmem((tokens + own * NEAR[1], rows), F32),
            vmem((tokens + own * NEAR[1], rows), F32),
            vmem((8, rows), F32),
            vmem((count, rows), BF16),
            vmem((count, rows), BF16),
            vmem((count, wide), BF16),
            vmem((count, lat), F32),
            vmem((PEERS, own, lat + 2 * rope), BF16),
            vmem((own, lat), BF16),
            vmem((own, rope), BF16),
            vmem((tokens, lat), BF16),
            vmem((rope, tokens), BF16),
            vmem((1, lat), F32),
            pltpu.SMEM((1, 1), jnp.int32),
            pltpu.SMEM((1, tokens), jnp.int32),
            pltpu.SMEM((1, 1), F32),
            vmem((count, wide), F32),
            vmem((LINE, LINE, own, wide), BF16),
            vmem((LINE, LINE, own, wide), BF16),
            vmem((LINE, own, wide), BF16),
            vmem((LINE, own, wide), BF16),
            vmem((1, lat), F32),
            vmem((PEERS, 1, lat), F32),
            vmem((1, lat), F32),
            vmem((PEERS, 1, lat), F32),
            pltpu.SemaphoreType.REGULAR,
            dma((12,)),
            dma((PEERS,)),
            dma((PEERS,)),
            dma((len(PARTS), LINE)),
            dma((len(PARTS), LINE)),
            dma((len(PARTS), LINE)),
            dma((len(PARTS), LINE)),
            dma((PEERS,)),
            dma((PEERS,)),
            dma((PEERS,)),
            dma((PEERS,)),
        ],
        compiler_params=pltpu.CompilerParams(
            collective_id=0, has_side_effects=True, vmem_limit_bytes=56 * 2**20
        ),
        name="grpo_backward",
    )(
        prefix_latent[0],
        prefix_rope[0],
        resp_latent[0, 0],
        resp_rope[0, 0].T,
        norm_gain[None],
        queries.reshape(rows, wide),
        cotangent.reshape(rows, lat),
        lengths,
        token_mask[0],
        rewards,
    )
    out = [value * SOFTMAX_SCALE for value in out]
    return (out[0][None], out[1][None], out[2][None, None], out[3].T[None, None], out[4][0])


def solution(mesh):
    placed = (
        P("prompt", "resp", None),
        P("prompt", "resp", None),
        P("prompt", "resp", None, None),
        P("prompt", "resp", None, None),
        P(),
        P("prompt", "resp", None, None, None),
        P("prompt", "resp", None, None, None),
        P("prompt", "resp"),
        P("prompt", "resp", None),
        P("prompt", "resp"),
    )
    return jax.shard_map(
        per_device,
        mesh=mesh,
        in_specs=placed,
        out_specs=(
            P("prompt", "resp", None),
            P("prompt", "resp", None),
            P("prompt", "resp", None, None),
            P("prompt", "resp", None, None),
            P(),
        ),
        check_vma=False,
    )
```

```python
import jax
import jax.numpy as jnp
from jax import lax
from jax.experimental import pallas as pl
from jax.experimental.pallas import tpu as pltpu
from jax.sharding import PartitionSpec as P

SOFTMAX_SCALE = 192.0 ** (-0.5)
LOG2E = 1.4426950408889634
NORM_EPSILON = 1e-06
NT = (((1,), (1,)), ((), ()))
LINE = 4
BLK = 512
UNROLL = 5
MESH = pl.DeviceIdType.MESH
F32, BF16 = jnp.float32, jnp.bfloat16


def normed_rows(raw):
    values = raw.astype(F32)
    inverse = lax.rsqrt(jnp.mean(values * values, axis=-1, keepdims=True) + NORM_EPSILON)
    return values * inverse, inverse


def norm_backward(upstream, normed, inverse, gain):
    scaled = upstream * gain
    expected = jnp.mean(scaled * normed, axis=-1, keepdims=True)
    return (scaled - normed * expected) * inverse


PEERS = LINE * LINE


def hops(offset):
    dz, dx = offset
    return 2 * min(dz, LINE - dz) + min(dx, LINE - dx)


OFFSETS = sorted(
    [(dz, dx) for dz in range(LINE) for dx in range(LINE)], key=lambda o: (o != (0, 0), o[0] > 0 and o[1] > 0, hops(o))
)
BACK = [OFFSETS.index(((LINE - dz) % LINE, (LINE - dx) % LINE)) for dz, dx in OFFSETS]
NEAR, FAR = (1, 7), (7, 16)
LATE = 13
PARTS = ((0, 256), (256, 512), (512, 576))


def kernel(
    pl_hbm, pr_hbm, rl_hbm, rr_hbm, gain_hbm, q_hbm, c_hbm, len_hbm, mask_hbm, rew_hbm,
    o_pl, o_pr, o_rl, o_rr, o_gain,
    q_v, c_v, powers_v, grad_soft_v, stats, p_st, d_st, keys, normed, gathered, pl_v, pr_v, rl_v, rr_v, gain_v,
    len_s, mask_s, rew_s, acc, send_x, recv_x, send_z, recv_z, gain_own, gain_a, gain_mid, gain_b,
    token, load_sem, g_send, g_recv, x_send, x_recv, z_send, z_recv, a_send, a_recv, b_send, b_recv,
):
    rows, lat = c_v.shape
    wide = q_v.shape[1]
    rope = wide - lat
    local = rl_v.shape[0]
    own = pl_v.shape[0]
    count = keys.shape[0]

    me = lax.axis_index("resp")
    prompt = lax.axis_index("prompt")
    my_z, my_x = me // LINE, lax.rem(me, LINE)

    def shift(value, step):
        return lax.rem(value + step, LINE)

    def same_prompt(position):
        dz, dx = OFFSETS[position]
        return {"resp": shift(my_z, dz) * LINE + shift(my_x, dx)}

    def same_plane(step):
        return {
            "prompt": shift(prompt // LINE, step // LINE) * LINE + lax.rem(prompt, LINE),
            "resp": my_z * LINE + shift(my_x, step % LINE),
        }

    def same_column(step):
        return {
            "prompt": prompt // LINE * LINE + shift(lax.rem(prompt, LINE), step // LINE),
            "resp": shift(my_z, step % LINE) * LINE + my_x,
        }

    my_y, my_low, my_core = prompt // LINE, lax.rem(prompt, LINE) // 2, lax.rem(prompt, 2)

    def near_prompt(dy, dlow, dcore):
        low, core = lax.rem(my_low + dlow, 2), lax.rem(my_core + dcore, 2)
        return {"prompt": shift(my_y, dy) * LINE + low * 2 + core}

    small = [
        pltpu.make_async_copy(src, dst, load_sem.at[i])
        for i, (src, dst) in enumerate(
            ((pl_hbm, pl_v), (pr_hbm, pr_v), (rew_hbm, rew_s), (rl_hbm, rl_v), (rr_hbm, rr_v),
             (gain_hbm, gain_v), (len_hbm, len_s), (mask_hbm, mask_s))
        )
    ]
    for copy in small:
        copy.start()

    barrier = pltpu.get_barrier_semaphore()
    targets = [same_prompt(OFFSETS.index(o)) for o in ((1, 0), (3, 0), (0, 2), (0, 1), (0, 3))]
    targets += [
        near_prompt(dy, dlow, dcore)
        for dy in (2, 1, 3, 0) for dlow in (1, 0) for dcore in (0, 1)
        if (dy > 0) != (dlow + dcore > 0)
    ]
    for target in targets:
        pl.semaphore_signal(barrier, inc=1, device_id=target, device_id_type=MESH)
    halves = tuple(pl.ds(start, rows // 2) for start in (0, rows // 2))
    big = [
        pltpu.make_async_copy(src.at[half], dst.at[half], load_sem.at[8 + 2 * i + j])
        for i, half in enumerate(halves) for j, (src, dst) in enumerate(((q_hbm, q_v), (c_hbm, c_v)))
    ]
    for copy in big:
        copy.start()
    for copy in small[:3]:
        copy.wait()

    reward = jnp.full((own, rope), rew_s[0, 0], F32)
    high = reward.astype(BF16)
    rest = reward - high.astype(F32)
    mid = rest.astype(BF16)
    low = (rest - mid.astype(F32)).astype(BF16)
    lane = lax.broadcasted_iota(jnp.int32, (own, rope), 1)
    terms = jnp.where(
        lane == 0, high.astype(F32), jnp.where(lane == 1, mid.astype(F32), jnp.where(lane == 2, low.astype(F32), 0.0))
    )
    gathered[0, :, :lat] = pl_v[...]
    gathered[0, :, lat:] = jnp.concatenate([pr_v[...].astype(F32), terms], axis=1).astype(BF16)

    pl.semaphore_wait(barrier, len(targets))
    gathers = {}

    def pass_on(block, offset):
        (dz, dx), (ez, ex) = OFFSETS[block], offset
        there = OFFSETS.index(((dz - ez) % LINE, (dx - ex) % LINE))
        copy = pltpu.make_async_remote_copy(
            src_ref=gathered.at[block], dst_ref=gathered.at[there],
            send_sem=g_send.at[there], recv_sem=g_recv.at[there],
            device_id=same_prompt(OFFSETS.index(offset)), device_id_type=MESH,
        )
        copy.start()
        gathers[there] = copy

    for dz in (1, 3):
        pass_on(0, (dz, 0))
    for dx in (2, 1, 3):
        pass_on(0, (0, dx))
    for copy in small[3:]:
        copy.wait()

    gain = gain_v[...]
    res_normed, res_inverse = normed_rows(rl_v[...])
    normed[:local, :] = res_normed
    keys[:local, :lat] = (res_normed * gain).astype(BF16)
    eye = (
        lax.broadcasted_iota(jnp.int32, (local, local), 0) == lax.broadcasted_iota(jnp.int32, (local, local), 1)
    ).astype(F32).astype(BF16)
    keys[:local, lat:] = lax.dot_general(eye, rr_v[...], NT, preferred_element_type=F32).astype(BF16)

    def place(first, last):
        lo, hi = local + first * own, local + last * own
        raw = gathered[first:last].reshape(hi - lo, lat + 2 * rope)
        rows_normed, rows_inverse = normed_rows(raw[:, :lat])
        normed[lo:hi, :] = rows_normed
        keys[lo:hi, :lat] = (rows_normed * gain).astype(BF16)
        keys[lo:hi, lat:] = raw[:, lat : lat + rope]
        return rows_normed, rows_inverse

    own_normed, own_inverse = place(0, 1)

    heads = rows // local
    half = rows // BLK // 2
    per_block = BLK // heads
    column = lax.broadcasted_iota(jnp.int32, (1, BLK), 1)
    key_at = lax.broadcasted_iota(jnp.int32, (local, BLK), 0)
    token_in = lax.broadcasted_iota(jnp.int32, (local, BLK), 1) // heads
    length = len_s[0, 0]
    groups = tuple((local + a * own, local + b * own) for a, b in (NEAR, FAR))
    groups = ((0, groups[0][0]),) + groups

    def score(group, first_block, last_block):
        lo, hi = groups[group]

        def step(block, carry):
            at = pl.ds(pl.multiple_of(block * BLK, BLK), BLK)
            first = block * per_block
            scores = lax.dot_general(keys[lo:hi, :], q_v[at, :], NT, preferred_element_type=F32)
            grad_soft = lax.dot_general(keys[lo:hi, :lat], c_v[at, :], NT, preferred_element_type=F32)
            if group == 0:
                visible = key_at <= token_in + first
                scores = jnp.concatenate([jnp.where(visible, scores[:local], -jnp.inf), scores[local:]], axis=0)
            top = jnp.max(scores, axis=0, keepdims=True)
            powers = jnp.exp2((scores - top) * (SOFTMAX_SCALE * LOG2E))
            total = jnp.sum(powers, axis=0, keepdims=True)
            weighted = jnp.sum(powers * grad_soft, axis=0, keepdims=True)
            if group < 2:
                powers_v[lo:hi, at] = powers
                grad_soft_v[lo:hi, at] = grad_soft
                stats[3 * group : 3 * group + 1, at] = top
                stats[3 * group + 1 : 3 * group + 2, at] = total
                stats[3 * group + 2 : 3 * group + 3, at] = weighted
                return carry
            live = jnp.zeros((1, BLK), F32)
            for i in range(per_block):
                weight = jnp.where((first + i < length) & (mask_s[0, first + i] > 0), 1.0, 0.0)
                live = jnp.where((column >= i * heads) & (column < (i + 1) * heads), weight, live)
            tops = (stats[0:1, at], stats[3:4, at], top)
            maximum = jnp.maximum(jnp.maximum(tops[0], tops[1]), top)
            scales = [jnp.exp2((t - maximum) * (SOFTMAX_SCALE * LOG2E)) for t in tops]
            inverse = 1.0 / (scales[0] * stats[1:2, at] + scales[1] * stats[4:5, at] + scales[2] * total)
            expected = (scales[0] * stats[2:3, at] + scales[1] * stats[5:6, at] + scales[2] * weighted) * inverse
            for g, (a, b) in enumerate(groups):
                part = powers if g == 2 else powers_v[a:b, at]
                grads = grad_soft if g == 2 else grad_soft_v[a:b, at]
                soft = part * (scales[g] * inverse * live)
                p_st[a:b, at] = soft.astype(BF16)
                d_st[a:b, at] = (soft * (grads - expected)).astype(BF16)
            return carry

        lax.fori_loop(first_block, last_block, step, 0, unroll=UNROLL)

    for copy in big[:2]:
        copy.wait()
    score(0, 0, half)
    for dz in (3, 1):
        block = OFFSETS.index((dz, 0))
        gathers[block].wait_recv()
        if dz == 3:
            pass_on(block, (1, 0))
        for dx in (2, 1, 3):
            pass_on(block, (0, dx))
    for copy in big[2:]:
        copy.wait()
    score(0, half, 2 * half)
    block = OFFSETS.index((2, 0))
    gathers[block].wait_recv()
    for dx in (2, 1, 3):
        pass_on(block, (0, dx))
    for dx in (1, 3, 2):
        gathers[OFFSETS.index((0, dx))].wait_recv()
    place(*NEAR)
    score(1, 0, 2 * half)
    for first, last in ((FAR[0], LATE), (LATE, FAR[1])):
        for p in range(first, last):
            gathers[p].wait_recv()
        place(first, last)
    for step in range(LINE, PEERS, LINE):
        pl.semaphore_signal(token, inc=1, device_id=same_plane(step), device_id_type=MESH)
        pl.semaphore_signal(token, inc=1, device_id=same_column(step), device_id_type=MESH)
    score(2, 0, 2 * half)
    for p in range(1, PEERS):
        gathers[p].wait_send()
    reward_rows = jnp.sum(gathered[:, :, lat:].astype(F32).reshape(PEERS * own, 2 * rope)[:, rope:], axis=0, keepdims=True)
    factor = jnp.sum(reward_rows, axis=1, keepdims=True) / (own * PEERS) - rew_s[0, 0]

    def contract(stored, values, lo, hi):
        return jnp.dot(stored[...], values[:, lo:hi], preferred_element_type=F32)

    along_x = []
    order = [[local + own * OFFSETS.index((dz, dx)) for dz in range(LINE)] for dx in range(LINE)]
    for part, (lo, hi) in enumerate(PARTS):
        total = contract(d_st, q_v, lo, hi)
        if hi <= lat:
            total = total + contract(p_st, c_v, lo, hi) * (1.0 / SOFTMAX_SCALE)
        total = total * factor
        acc[:, lo:hi] = total
        if hi <= lat:
            gain_own[:, lo:hi] = jnp.sum(total * normed[:, lo:hi], axis=0, keepdims=True)
        if hi == lat:
            pl.semaphore_wait(token, 2 * (LINE - 1))
            near = []
            for step in range(1, PEERS):
                copy = pltpu.make_async_remote_copy(
                    src_ref=gain_own, dst_ref=gain_a.at[step],
                    send_sem=a_send.at[step], recv_sem=a_recv.at[step],
                    device_id=same_plane(step), device_id_type=MESH,
                )
                copy.start()
                near.append(copy)
        for dx in range(1, LINE):
            for dz in range(LINE):
                at = order[dx][dz]
                send_x[dx, dz, :, lo:hi] = total[at : at + own].astype(BF16)
        started = []
        for dx in (2, 1, 3):
            copy = pltpu.make_async_remote_copy(
                src_ref=send_x.at[dx, :, :, lo:hi], dst_ref=recv_x.at[dx, :, :, lo:hi],
                send_sem=x_send.at[part, dx], recv_sem=x_recv.at[part, dx],
                device_id=same_prompt(OFFSETS.index((0, dx))), device_id_type=MESH,
            )
            copy.start()
            started.append(copy)
        along_x.append(started)

    along_z = []
    for part, (lo, hi) in enumerate(PARTS):
        if part == len(PARTS) - 1:
            for copy in near:
                copy.wait()
            total_gain = gain_own[...]
            for step in range(1, PEERS):
                total_gain = total_gain + gain_a[step]
            gain_mid[...] = total_gain
            far = []
            for step in range(1, PEERS):
                copy = pltpu.make_async_remote_copy(
                    src_ref=gain_mid, dst_ref=gain_b.at[step],
                    send_sem=b_send.at[step], recv_sem=b_recv.at[step],
                    device_id=same_column(step), device_id_type=MESH,
                )
                copy.start()
                far.append(copy)
        for copy in along_x[part]:
            copy.wait()
        for dz in range(LINE):
            at = order[0][dz]
            total = acc[at : at + own, lo:hi]
            for dx in range(1, LINE):
                total = total + recv_x[dx, dz, :, lo:hi].astype(F32)
            if dz == 0:
                acc[at : at + own, lo:hi] = total
            else:
                send_z[dz, :, lo:hi] = total.astype(BF16)
        for dz in (2, 1, 3):
            copy = pltpu.make_async_remote_copy(
                src_ref=send_z.at[dz, :, lo:hi], dst_ref=recv_z.at[dz, :, lo:hi],
                send_sem=z_send.at[part, dz], recv_sem=z_recv.at[part, dz],
                device_id=same_prompt(OFFSETS.index((dz, 0))), device_id_type=MESH,
            )
            copy.start()
            along_z.append(copy)

    o_rl[...] = norm_backward(acc[:local, :lat], res_normed, res_inverse, gain)
    o_rr[...] = acc[:local, lat:].T
    for copy in along_z:
        copy.wait()
    total = acc[local : local + own, :]
    for dz in range(1, LINE):
        total = total + recv_z[dz].astype(F32)
    o_pl[...] = norm_backward(total[:, :lat], own_normed, own_inverse, gain)
    o_pr[...] = total[:, lat:]

    for copy in far:
        copy.wait()
    total_gain = gain_mid[...]
    for step in range(1, PEERS):
        total_gain = total_gain + gain_b[step]
    o_gain[...] = total_gain


def per_device(
    prefix_latent, prefix_rope, resp_latent, resp_rope, norm_gain, queries, cotangent, lengths, token_mask, rewards
):
    tokens, heads, wide = queries.shape[2:]
    lat = cotangent.shape[-1]
    rope = wide - lat
    own = prefix_latent.shape[1]
    rows = tokens * heads
    count = own * PEERS + tokens
    vmem, dma = pltpu.VMEM, pltpu.SemaphoreType.DMA
    shapes = ((own, lat), (own, rope), (tokens, lat), (rope, tokens), (1, lat))
    out = pl.pallas_call(
        kernel,
        out_shape=tuple(pltpu.VMEM(s, F32) for s in shapes),
        in_specs=[pl.BlockSpec(memory_space=pltpu.HBM)] * 10,
        out_specs=[pl.BlockSpec(memory_space=pltpu.VMEM)] * 5,
        scratch_shapes=[
            vmem((rows, wide), BF16),
            vmem((rows, lat), BF16),
            vmem((tokens + own * NEAR[1], rows), F32),
            vmem((tokens + own * NEAR[1], rows), F32),
            vmem((8, rows), F32),
            vmem((count, rows), BF16),
            vmem((count, rows), BF16),
            vmem((count, wide), BF16),
            vmem((count, lat), F32),
            vmem((PEERS, own, lat + 2 * rope), BF16),
            vmem((own, lat), BF16),
            vmem((own, rope), BF16),
            vmem((tokens, lat), BF16),
            vmem((rope, tokens), BF16),
            vmem((1, lat), F32),
            pltpu.SMEM((1, 1), jnp.int32),
            pltpu.SMEM((1, tokens), jnp.int32),
            pltpu.SMEM((1, 1), F32),
            vmem((count, wide), F32),
            vmem((LINE, LINE, own, wide), BF16),
            vmem((LINE, LINE, own, wide), BF16),
            vmem((LINE, own, wide), BF16),
            vmem((LINE, own, wide), BF16),
            vmem((1, lat), F32),
            vmem((PEERS, 1, lat), F32),
            vmem((1, lat), F32),
            vmem((PEERS, 1, lat), F32),
            pltpu.SemaphoreType.REGULAR,
            dma((12,)),
            dma((PEERS,)),
            dma((PEERS,)),
            dma((len(PARTS), LINE)),
            dma((len(PARTS), LINE)),
            dma((len(PARTS), LINE)),
            dma((len(PARTS), LINE)),
            dma((PEERS,)),
            dma((PEERS,)),
            dma((PEERS,)),
            dma((PEERS,)),
        ],
        compiler_params=pltpu.CompilerParams(
            collective_id=0, has_side_effects=True, vmem_limit_bytes=56 * 2**20
        ),
        name="grpo_backward",
    )(
        prefix_latent[0],
        prefix_rope[0],
        resp_latent[0, 0],
        resp_rope[0, 0].T,
        norm_gain[None],
        queries.reshape(rows, wide),
        cotangent.reshape(rows, lat),
        lengths,
        token_mask[0],
        rewards,
    )
    out = [value * SOFTMAX_SCALE for value in out]
    return (out[0][None], out[1][None], out[2][None, None], out[3].T[None, None], out[4][0])


def solution(mesh):
    placed = (
        P("prompt", "resp", None),
        P("prompt", "resp", None),
        P("prompt", "resp", None, None),
        P("prompt", "resp", None, None),
        P(),
        P("prompt", "resp", None, None, None),
        P("prompt", "resp", None, None, None),
        P("prompt", "resp"),
        P("prompt", "resp", None),
        P("prompt", "resp"),
    )
    return jax.shard_map(
        per_device,
        mesh=mesh,
        in_specs=placed,
        out_specs=(
            P("prompt", "resp", None),
            P("prompt", "resp", None),
            P("prompt", "resp", None, None),
            P("prompt", "resp", None, None),
            P(),
        ),
        check_vma=False,
    )
```
